32 devices in a mesh: ctx: 16 (over z, y, x), tp: 2 (over core).
Axes of the slice: x: 2, y: 2, z: 4, core: 2. Of those that a mesh axis runs over, the one named last changes fastest.
Arguments:
- tokens: bfloat16 [2048, 1024], P('ctx', 'tp'), may hold values from -6 to 6
- segment_ids: int32 [2048], P('ctx'), may hold values from 0 to 2, as said below
- ln1_gain: float32 [1024], replicated, may hold values from 0.25 to 1.75
- ln1_bias: float32 [1024], replicated, may hold values from -4 to 4
- w_qkv: bfloat16 [3, 1024, 1024], P(None, None, 'tp'), may hold values from -0.1875 to 0.1875
- b_qv: float32 [2, 1024], P(None, 'tp'), may hold values from -6 to 6
- w_out: bfloat16 [1024, 1024], P('tp'), may hold values from -0.375 to 0.375
- b_out: float32 [1024], P('tp'), may hold values from -6 to 6
- ln2_gain: float32 [1024], replicated, may hold values from 0.25 to 1.75
- ln2_bias: float32 [1024], replicated, may hold values from -4 to 4
- w_up: bfloat16 [1024, 4096], P(None, 'tp'), may hold values from -0.1875 to 0.1875
- b_up: float32 [4096], P('tp'), may hold values from -6 to 6
- w_down: bfloat16 [4096, 1024], P('tp'), may hold values from -0.09375 to 0.09375
- b_down: float32 [1024], P('tp'), may hold values from -6 to 6
- cotangent: bfloat16 [2048, 1024], P('ctx', 'tp'), may hold values from -6 to 6
Outputs:
- mixed: bfloat16 [2048, 1024], P('ctx', 'tp')
- input_grad: bfloat16 [2048, 1024], P('ctx', 'tp')
- ln1_gain_grad: float32 [1024], P(('tp', 'ctx'))
- ln1_bias_grad: float32 [1024], P(('tp', 'ctx'))
- w_qkv_grad: float32 [3, 1024, 1024], P(None, 'ctx', 'tp')
- b_qv_grad: float32 [2, 1024], P(None, ('tp', 'ctx'))
- w_out_grad: float32 [1024, 1024], P('tp', 'ctx')
- b_out_grad: float32 [1024], P(('tp', 'ctx'))
- ln2_gain_grad: float32 [1024], P(('tp', 'ctx'))
- ln2_bias_grad: float32 [1024], P(('tp', 'ctx'))
- w_up_grad: float32 [1024, 4096], P('ctx', 'tp')
- b_up_grad: float32 [4096], P(('tp', 'ctx'))
- w_down_grad: float32 [4096, 1024], P('tp', 'ctx')
- b_down_grad: float32 [1024], P(('tp', 'ctx'))
The draws below stay inside these ranges and needn't reach their ends.
Inputs may be any that keep to these rules, and one draw needn't show every extreme that they name: `segment_ids`: document numbers never fall along the tokens; documents 0 and 2 hold 1 to 64 tokens each, so document 1 starts in the first block of 128 tokens and ends in the last one.
All inputs are finite; a program needn't handle non-finite values.
Results may differ from the reference program's by a relative error of at most 0.039.
Values may be sent and summed in bfloat16 or wider, within the bound.
No kernel may reach another device: no remote copies, remote signals or barrier semaphores. Data moves between devices by JAX's collectives and lax.ppermute only.
A program may use at most 128 MiB of HBM per device.

```python
import math
from functools import partial
import jax
import jax.numpy as jnp
from jax import lax

D = 1024
HEADS = 16
HDIM = 64
FF = 4096
TOK_DEV = 128
TOKENS = 2048


def draw_segment_ids(key, part):
    key = jax.random.fold_in(key, 17)
    first_key, last_key = jax.random.split(key)
    head_len = jax.random.randint(first_key, (), 1, TOK_DEV // 2 + 1, dtype=jnp.int32)
    tail_len = jax.random.randint(last_key, (), 1, TOK_DEV // 2 + 1, dtype=jnp.int32)
    position = jnp.arange(TOKENS, dtype=jnp.int32)
    return (position >= head_len).astype(jnp.int32) + (position >= TOKENS - tail_len).astype(jnp.int32)


def with_spikes(entries, own_key, source, target, shards_of, factor):
    def block_of(dim):
        return (jnp.arange(entries.shape[dim]) // (entries.shape[dim] // shards_of)).reshape((-1,) + (1,) * (entries.ndim - 1 - dim))

    one_side = jax.random.permutation(own_key, shards_of)[block_of(target)]
    second = (block_of(target) + shards_of // 2) % shards_of
    return jnp.where((block_of(source) == one_side) | (block_of(source) == second), factor * entries, entries)


def steps_of(rng, dims, shards, low, high):
    level = 1.0
    for axis_at, shards_of in shards:
        heights = jax.random.uniform(jax.random.fold_in(jax.random.fold_in(rng, 6), axis_at), (shards_of,), jnp.float32, low / len(shards), high / len(shards))
        level = level * jnp.repeat(jnp.exp(heights), dims[axis_at] // shards_of).reshape((-1,) + (1,) * (len(dims) - 1 - axis_at))
    return level


def normal_values(rng, dims, deviation, bound, pieces=(), held_as=jnp.bfloat16):
    array = deviation * jax.random.normal(rng, dims, jnp.float32)
    if pieces:
        array = array * steps_of(rng, dims, pieces, -0.22, 0.18)
    return jnp.clip(array, -bound, bound).astype(held_as)


def noise_with(rng, dims, width, most, cuts, heavy, held_as=jnp.bfloat16):
    array = width * jax.random.normal(rng, dims, jnp.float32)
    if cuts:
        array = array * steps_of(rng, dims, cuts, -0.22, 0.18)
    return jnp.clip(with_spikes(array, jax.random.fold_in(rng, 3), *heavy), -most, most).astype(held_as)


def setup_inputs(seed: int = 0) -> dict:
    splits = jax.random.split(jax.random.key(seed), 16)
    tokens = normal_values(splits[0], (TOKENS, D), 1.0, 6.0, ((0, 16), (1, 2)))
    segment_ids = draw_segment_ids(jax.random.fold_in(splits[15], 71), 0)
    ln1_gain = jnp.clip(1.0 + 0.15 * jax.random.normal(splits[2], (D,), jnp.float32), 0.25, 1.75)
    ln1_bias = normal_values(splits[3], (D,), 0.3, 4.0, (), jnp.float32)
    w_qkv = normal_values(splits[4], (3, D, D), D ** -0.5, 0.1875, ((2, 2),))
    b_qv = normal_values(splits[5], (2, D), 0.5, 6.0, ((1, 2),), jnp.float32)
    w_out = normal_values(splits[6], (D, D), (D // 4) ** -0.5, 0.375, ((0, 2),))
    b_out = normal_values(splits[7], (D,), 0.5, 6.0, ((0, 2),), jnp.float32)
    ln2_gain = jnp.clip(1.0 + 0.15 * jax.random.normal(splits[8], (D,), jnp.float32), 0.25, 1.75)
    ln2_bias = normal_values(splits[9], (D,), 0.3, 4.0, (), jnp.float32)
    w_up = normal_values(splits[10], (D, FF), D ** -0.5, 0.1875, ((1, 2),))
    b_up = normal_values(splits[11], (FF,), 0.5, 6.0, ((0, 2),), jnp.float32)
    w_down = normal_values(splits[12], (FF, D), FF ** -0.5, 0.09375, ((0, 2),))
    b_down = normal_values(splits[13], (D,), 0.5, 6.0, ((0, 2),), jnp.float32)
    cotangent = noise_with(splits[14], (TOKENS, D), 1.0, 6.0, ((0, 16), (1, 2)), (0, 1, 16, 2.0))
    return dict(tokens=tokens, segment_ids=segment_ids, ln1_gain=ln1_gain, ln1_bias=ln1_bias, w_qkv=w_qkv, b_qv=b_qv, w_out=w_out, b_out=b_out, ln2_gain=ln2_gain, ln2_bias=ln2_bias, w_up=w_up, b_up=b_up, w_down=w_down, b_down=b_down, cotangent=cotangent)


highest = lax.Precision.HIGHEST

@jax.custom_vjp
def low(v):
    return lax.optimization_barrier(v.astype(jnp.bfloat16)).astype(jnp.float32)

@jax.custom_vjp
def low_back(v):
    return v

def low_keep(v):
    return (low(v), None)

def low_pass(kept, grad):
    return (grad,)

def back_keep(v):
    return (v, None)

def back_low(kept, grad):
    return (low(grad),)
low.defvjp(low_keep, low_pass)
low_back.defvjp(back_keep, back_low)

def layer_norm(values, gain, bias):
    center = values - lax.optimization_barrier(jnp.mean(values, axis=-1, keepdims=True))
    spread = lax.optimization_barrier(jnp.mean(center * center, axis=-1, keepdims=True))
    return center * lax.rsqrt(spread + 1e-05) * gain + bias

def attend_block(query_block, first_row, key_heads, value_heads, segment_ids, slopes):
    row_count = query_block.shape[0]
    query_pos = first_row + jnp.arange(row_count, dtype=jnp.int32)
    key_pos = jnp.arange(key_heads.shape[0], dtype=jnp.int32)
    query_seg = lax.dynamic_slice_in_dim(segment_ids, first_row, row_count)
    logits = jnp.einsum('qhd,khd->hqk', query_block, key_heads, precision=highest) / math.sqrt(HDIM)
    distance = (key_pos[None, :] - query_pos[:, None]).astype(jnp.float32)
    allowed = (key_pos[None, :] <= query_pos[:, None]) & (segment_ids[None, :] == query_seg[:, None])
    score = jnp.where(allowed[None], logits + slopes[:, None, None] * distance[None], -1e+30)
    score = low_back(score)
    shifted = jnp.exp(score - lax.optimization_barrier(jnp.max(score, axis=-1, keepdims=True)))
    weights = shifted / lax.optimization_barrier(jnp.sum(shifted, axis=-1, keepdims=True))
    return jnp.einsum('hqk,khd->qhd', low(weights), value_heads, precision=highest)

def attention(query, key_rows, value_rows, segment_ids):
    block_len = math.gcd(TOKENS, 256)
    query_blocks = query.reshape(TOKENS // block_len, block_len, HEADS, HDIM)
    key_heads = key_rows.reshape(TOKENS, HEADS, HDIM)
    value_heads = value_rows.reshape(TOKENS, HEADS, HDIM)
    starts = jnp.arange(TOKENS // block_len, dtype=jnp.int32) * block_len
    slopes = jnp.exp2(-8.0 * jnp.arange(1, HEADS + 1).astype(jnp.float32) / HEADS)
    runner = jax.checkpoint(attend_block)
    result = lax.map(lambda packed_item: runner(packed_item[0], packed_item[1], key_heads, value_heads, segment_ids, slopes), (query_blocks, starts))
    return result.reshape(TOKENS, D)

def forward(segment_ids, tokens, gain_one, bias_one, w_qkv, b_qv, w_out, b_out, gain_two, bias_two, w_up, b_up, w_down, b_down):
    hidden_one = low(layer_norm(tokens, gain_one, bias_one))
    query = low(low_back(jnp.dot(hidden_one, w_qkv[0], precision=highest) + b_qv[0]))
    key_rows = low(low_back(jnp.dot(hidden_one, w_qkv[1], precision=highest)))
    value_rows = low(low_back(jnp.dot(hidden_one, w_qkv[2], precision=highest) + b_qv[1]))
    attended = low(low_back(attention(query, key_rows, value_rows, segment_ids)))
    middle = tokens + low_back(jnp.dot(attended, w_out, precision=highest)) + b_out
    hidden_two = low(layer_norm(low(middle), gain_two, bias_two))
    pre_act = low_back(jnp.dot(hidden_two, w_up, precision=highest) + b_up)
    activated = low(jax.nn.gelu(pre_act, approximate=True))
    return middle + jnp.dot(activated, w_down, precision=highest) + b_down

def reference(tokens, segment_ids, ln1_gain, ln1_bias, w_qkv, b_qv, w_out, b_out, ln2_gain, ln2_bias, w_up, b_up, w_down, b_down, cotangent):
    params = (tokens.astype(jnp.float32), ln1_gain, ln1_bias, w_qkv.astype(jnp.float32), b_qv, w_out.astype(jnp.float32), b_out, ln2_gain, ln2_bias, w_up.astype(jnp.float32), b_up, w_down.astype(jnp.float32), b_down)
    mixed, backward = jax.vjp(partial(forward, segment_ids), *params)
    grads = backward(cotangent.astype(jnp.float32))
    return (mixed.astype(jnp.bfloat16), grads[0].astype(jnp.bfloat16), grads[1], grads[2], grads[3], grads[4], grads[5], grads[6], grads[7], grads[8], grads[9], grads[10], grads[11], grads[12])
```

```python
import functools
import math

import jax
import jax.numpy as jnp
from jax import lax
from jax.experimental import pallas as pl
from jax.experimental.pallas import tpu as pltpu
from jax.sharding import PartitionSpec as P

HEADS = 16
HDIM = 64


norm_eps = 1e-05
mask_fill = -1e30
score_block = 512

HALF = 64
SOURCES = 4
QUERIES = SOURCES * HALF
SEG_ROW = 5 * HDIM // 2
FWD_ROWS = SEG_ROW + 16
BACK_ROWS = SEG_ROW + 3 * HDIM // 2
GELU_A = math.sqrt(2.0 / math.pi)
GELU_B = 0.044715


def head_slopes(first_head, head_count):
    index_list = first_head + jnp.arange(head_count, dtype=jnp.int32)
    return jnp.exp2(-8.0 * (index_list + 1).astype(jnp.float32) / HEADS)


def pair_scores(query_heads, query_pos, query_seg, key_heads, key_pos, key_seg, slopes):
    logits = jnp.einsum(
        "qhd,khd->hqk", query_heads, key_heads, preferred_element_type=jnp.float32
    ) / math.sqrt(HDIM)
    distance = (key_pos[None, :] - query_pos[:, None]).astype(jnp.float32)
    allowed = (key_pos[None, :] <= query_pos[:, None]) & (key_seg[None, :] == query_seg[:, None])
    return (
        jnp.where(allowed[None], logits + slopes[:, None, None] * distance[None], mask_fill),
        allowed,
    )


def block_grads(
    query_heads,
    query_pos,
    query_seg,
    grad_heads,
    lse_rows,
    delta_rows,
    key_heads,
    value_heads,
    key_pos,
    key_seg,
    slopes,
):
    score, allowed = pair_scores(
        query_heads, query_pos, query_seg, key_heads, key_pos, key_seg, slopes
    )
    prob = jnp.where(allowed[None], jnp.exp(score - lse_rows.T[:, :, None]), 0.0)
    grad_prob = jnp.einsum(
        "qhd,khd->hqk", grad_heads, value_heads, preferred_element_type=jnp.float32
    )
    grad_score = (prob * (grad_prob - delta_rows.T[:, :, None])).astype(jnp.bfloat16)
    return (prob.astype(jnp.bfloat16), grad_score)


def over_blocks(row_count, step_fn, state_now):
    return lax.fori_loop(
        0,
        row_count // score_block,
        lambda number, inner_state: step_fn(number * score_block, score_block, inner_state),
        state_now,
    )


def seg_at(seg_array, where_row):
    return lax.dynamic_slice_in_dim(seg_array, where_row, 1)[0]


def gather_features(local_rows):
    return lax.all_gather(local_rows, "tp", axis=1, tiled=True)


def norm_stats(full_rows):
    center = full_rows - jnp.mean(full_rows, axis=-1, keepdims=True)
    inverse = lax.rsqrt(jnp.mean(center * center, axis=-1, keepdims=True) + norm_eps)
    return (center * inverse, inverse)


def norm_backward(part_grad, normed, inverse, gain, tp_rank, local_width):
    offset = tp_rank * local_width
    whole_grad = lax.psum(part_grad.astype(jnp.bfloat16), "tp").astype(jnp.float32)
    scaled = whole_grad * gain
    mean_one = jnp.mean(scaled, axis=-1, keepdims=True)
    mean_two = jnp.mean(scaled * normed, axis=-1, keepdims=True)
    input_grad = lax.dynamic_slice_in_dim(
        inverse * (scaled - mean_one - normed * mean_two), offset, local_width, 1
    )
    share_grad = lax.dynamic_slice_in_dim(whole_grad, offset, local_width, 1)
    normed_share = lax.dynamic_slice_in_dim(normed, offset, local_width, 1)
    gain_grad = jnp.sum(share_grad * normed_share, axis=0)
    bias_grad = jnp.sum(share_grad, axis=0)
    return (input_grad, gain_grad, bias_grad)


def on_device(
    tokens,
    segment_ids,
    ln1_gain,
    ln1_bias,
    w_qkv,
    b_qv,
    w_out,
    b_out,
    ln2_gain,
    ln2_bias,
    w_up,
    b_up,
    w_down,
    b_down,
    cotangent,
):
    local_rows, local_width = tokens.shape
    heads_local = local_width // HDIM
    tp_rank = lax.axis_index("tp")
    ctx_rank = lax.axis_index("ctx")
    slopes = head_slopes(tp_rank * heads_local, heads_local)
    own_pos = ctx_rank * local_rows + jnp.arange(local_rows, dtype=jnp.int32)
    own_first_seg = segment_ids[0]
    own_last_seg = segment_ids[-1]
    full_in = gather_features(tokens)
    normed_one, inverse_one = norm_stats(full_in.astype(jnp.float32))
    hidden_one = (normed_one * ln1_gain + ln1_bias).astype(jnp.bfloat16)
    projected = jnp.einsum("td,cde->cte", hidden_one, w_qkv, preferred_element_type=jnp.float32)
    query_rows = (projected[0] + b_qv[0]).astype(jnp.bfloat16)
    key_rows = projected[1].astype(jnp.bfloat16)
    value_rows = (projected[2] + b_qv[1]).astype(jnp.bfloat16)
    query_heads = query_rows.reshape(local_rows, heads_local, HDIM)
    key_heads = key_rows.reshape(local_rows, heads_local, HDIM)
    value_heads = value_rows.reshape(local_rows, heads_local, HDIM)
    start_state = (
        jnp.full((heads_local, local_rows), mask_fill, jnp.float32),
        jnp.zeros((heads_local, local_rows), jnp.float32),
        jnp.zeros((heads_local, local_rows, HDIM), jnp.float32),
    )
    piece_keys = lax.all_gather(key_rows, "ctx", axis=0, tiled=True)
    piece_values = lax.all_gather(value_rows, "ctx", axis=0, tiled=True)
    piece_seg = lax.all_gather(segment_ids, "ctx", axis=0, tiled=True)

    def forward_one_block(offset, size_each, inner_state):

        def attend(running):
            high_now, total_now, acc_now = running
            block_keys = lax.dynamic_slice_in_dim(piece_keys, offset, size_each).reshape(
                size_each, heads_local, HDIM
            )
            block_values = lax.dynamic_slice_in_dim(piece_values, offset, size_each).reshape(
                size_each, heads_local, HDIM
            )
            block_seg = lax.dynamic_slice_in_dim(piece_seg, offset, size_each)
            key_pos = offset + jnp.arange(size_each, dtype=jnp.int32)
            score, allowed = pair_scores(
                query_heads, own_pos, segment_ids, block_keys, key_pos, block_seg, slopes
            )
            high_new = jnp.maximum(high_now, jnp.max(score, axis=-1))
            weights = jnp.where(allowed[None], jnp.exp(score - high_new[:, :, None]), 0.0)
            factor = jnp.exp(high_now - high_new)
            total_new = total_now * factor + jnp.sum(weights, axis=-1)
            acc_new = acc_now * factor[:, :, None] + jnp.einsum(
                "hqk,khd->hqd",
                weights.astype(jnp.bfloat16),
                block_values,
                preferred_element_type=jnp.float32,
            )
            return (high_new, total_new, acc_new)

        needed = (offset <= own_pos[-1]) & (
            seg_at(piece_seg, offset + size_each - 1) >= own_first_seg
        )
        return lax.cond(needed, attend, lambda running: running, inner_state)

    high_fin, total_fin, acc_fin = over_blocks(piece_keys.shape[0], forward_one_block, start_state)
    attn_raw = jnp.transpose(acc_fin / total_fin[:, :, None], (1, 0, 2)).reshape(
        local_rows, local_width
    )
    lse_rows = (high_fin + jnp.log(total_fin)).T
    attn_low = attn_raw.astype(jnp.bfloat16)
    attn_share = lax.psum_scatter(
        jnp.dot(attn_low, w_out, preferred_element_type=jnp.float32).astype(jnp.bfloat16),
        "tp",
        scatter_dimension=1,
        tiled=True,
    ).astype(jnp.float32)
    middle = tokens.astype(jnp.float32) + attn_share + b_out
    full_mid = gather_features(middle.astype(jnp.bfloat16))
    normed_two, inverse_two = norm_stats(full_mid.astype(jnp.float32))
    hidden_two = (normed_two * ln2_gain + ln2_bias).astype(jnp.bfloat16)
    pre_act = jnp.dot(hidden_two, w_up, preferred_element_type=jnp.float32) + b_up
    gelu_out, gelu_back = jax.vjp(
        lambda pre_value: jax.nn.gelu(pre_value, approximate=True), pre_act
    )
    activated = gelu_out.astype(jnp.bfloat16)
    mlp_share = lax.psum_scatter(
        jnp.dot(activated, w_down, preferred_element_type=jnp.float32).astype(jnp.bfloat16),
        "tp",
        scatter_dimension=1,
        tiled=True,
    ).astype(jnp.float32)
    output = middle + mlp_share + b_down
    contract_rows = (((0,), (0,)), ((), ()))
    contract_cols = (((1,), (1,)), ((), ()))
    out_grad = cotangent.astype(jnp.float32)
    full_cot = gather_features(cotangent)
    grad_down = lax.dot_general(
        activated, full_cot, contract_rows, preferred_element_type=jnp.float32
    )
    grad_act = lax.dot_general(full_cot, w_down, contract_cols, preferred_element_type=jnp.float32)
    grad_pre = gelu_back(grad_act)[0].astype(jnp.bfloat16)
    grad_bup = jnp.sum(grad_pre.astype(jnp.float32), axis=0)
    grad_up = lax.dot_general(
        hidden_two, grad_pre, contract_rows, preferred_element_type=jnp.float32
    )
    part_two = lax.dot_general(grad_pre, w_up, contract_cols, preferred_element_type=jnp.float32)
    grad_mid_norm, grad_gain_two, grad_bias_two = norm_backward(
        part_two, normed_two, inverse_two, ln2_gain, tp_rank, local_width
    )
    grad_middle = out_grad + grad_mid_norm
    grad_bdown = jnp.sum(out_grad, axis=0)
    grad_bout = jnp.sum(grad_middle, axis=0)
    full_back = gather_features(grad_middle.astype(jnp.bfloat16))
    grad_wout = lax.dot_general(
        attn_low, full_back, contract_rows, preferred_element_type=jnp.float32
    )
    grad_attn = lax.dot_general(
        full_back, w_out, contract_cols, preferred_element_type=jnp.float32
    ).astype(jnp.bfloat16)
    grad_heads = grad_attn.reshape(local_rows, heads_local, HDIM)
    delta_rows = jnp.sum(
        grad_heads.astype(jnp.float32) * attn_raw.reshape(local_rows, heads_local, HDIM), axis=-1
    )
    query_zero = jnp.zeros((local_rows, heads_local, HDIM), jnp.float32)
    back_state = (query_zero,)
    backward_piece_keys = lax.all_gather(key_rows, "ctx", axis=0, tiled=True)
    backward_piece_values = lax.all_gather(value_rows, "ctx", axis=0, tiled=True)
    backward_piece_seg = lax.all_gather(segment_ids, "ctx", axis=0, tiled=True)

    def backward_one_block(offset, size_each, inner_state):

        def backward_work(running):
            block_keys = lax.dynamic_slice_in_dim(backward_piece_keys, offset, size_each).reshape(
                size_each, heads_local, HDIM
            )
            block_values = lax.dynamic_slice_in_dim(
                backward_piece_values, offset, size_each
            ).reshape(size_each, heads_local, HDIM)
            block_seg = lax.dynamic_slice_in_dim(backward_piece_seg, offset, size_each)
            key_pos = offset + jnp.arange(size_each, dtype=jnp.int32)
            prob_low, grad_score = block_grads(
                query_heads,
                own_pos,
                segment_ids,
                grad_heads,
                lse_rows,
                delta_rows,
                block_keys,
                block_values,
                key_pos,
                block_seg,
                slopes,
            )
            query_acc = running[0] + jnp.einsum(
                "hqk,khd->qhd", grad_score, block_keys, preferred_element_type=jnp.float32
            ) / math.sqrt(HDIM)
            return (query_acc,)

        needed = (offset <= own_pos[-1]) & (
            seg_at(backward_piece_seg, offset + size_each - 1) >= own_first_seg
        )
        return lax.cond(needed, backward_work, lambda running: running, inner_state)

    back_result = over_blocks(backward_piece_keys.shape[0], backward_one_block, back_state)
    query_grad = back_result[0].reshape(local_rows, local_width)
    piece_query = lax.all_gather(query_rows, "ctx", axis=0, tiled=True)
    piece_grad = lax.all_gather(grad_attn, "ctx", axis=0, tiled=True)
    piece_lse = lax.all_gather(lse_rows.astype(jnp.bfloat16), "ctx", axis=0, tiled=True).astype(
        jnp.float32
    )
    piece_delta = lax.all_gather(delta_rows.astype(jnp.bfloat16), "ctx", axis=0, tiled=True).astype(
        jnp.float32
    )
    owner_piece_seg = lax.all_gather(segment_ids, "ctx", axis=0, tiled=True)

    def owner_one_block(offset, size_each, inner_state):

        def owner_work(running):
            key_acc, value_acc = running
            block_query = lax.dynamic_slice_in_dim(piece_query, offset, size_each).reshape(
                size_each, heads_local, HDIM
            )
            block_grad = lax.dynamic_slice_in_dim(piece_grad, offset, size_each).reshape(
                size_each, heads_local, HDIM
            )
            block_lse = lax.dynamic_slice_in_dim(piece_lse, offset, size_each)
            block_delta = lax.dynamic_slice_in_dim(piece_delta, offset, size_each)
            block_seg = lax.dynamic_slice_in_dim(owner_piece_seg, offset, size_each)
            query_pos = offset + jnp.arange(size_each, dtype=jnp.int32)
            prob_low, grad_score = block_grads(
                block_query,
                query_pos,
                block_seg,
                block_grad,
                block_lse,
                block_delta,
                key_heads,
                value_heads,
                own_pos,
                segment_ids,
                slopes,
            )
            key_acc = key_acc + jnp.einsum(
                "hqk,qhd->khd", grad_score, block_query, preferred_element_type=jnp.float32
            ) / math.sqrt(HDIM)
            value_acc = value_acc + jnp.einsum(
                "hqk,qhd->khd", prob_low, block_grad, preferred_element_type=jnp.float32
            )
            return (key_acc, value_acc)

        needed = (offset + size_each - 1 >= own_pos[0]) & (
            seg_at(owner_piece_seg, offset) <= own_last_seg
        )
        return lax.cond(needed, owner_work, lambda running: running, inner_state)

    key_acc, value_acc = over_blocks(
        piece_query.shape[0], owner_one_block, (query_zero, query_zero)
    )
    key_grad = key_acc.reshape(local_rows, local_width)
    value_grad = value_acc.reshape(local_rows, local_width)
    query_low = query_grad.astype(jnp.bfloat16)
    key_low = key_grad.astype(jnp.bfloat16)
    value_low = value_grad.astype(jnp.bfloat16)
    grad_bqv = jnp.stack(
        (
            jnp.sum(query_low.astype(jnp.float32), axis=0),
            jnp.sum(value_low.astype(jnp.float32), axis=0),
        )
    )
    stacked_grads = jnp.stack((query_low, key_low, value_low))
    grad_qkv = jnp.einsum(
        "td,cte->cde", hidden_one, stacked_grads, preferred_element_type=jnp.float32
    )
    part_one = jnp.einsum("cte,cde->td", stacked_grads, w_qkv, preferred_element_type=jnp.float32)
    grad_in_norm, grad_gain_one, grad_bias_one = norm_backward(
        part_one, normed_one, inverse_one, ln1_gain, tp_rank, local_width
    )
    input_grad = (grad_middle + grad_in_norm).astype(jnp.bfloat16)
    reduced = (
        lax.psum_scatter(
            grad_gain_one.astype(jnp.bfloat16), "ctx", scatter_dimension=0, tiled=True
        ).astype(jnp.float32),
        lax.psum_scatter(
            grad_bias_one.astype(jnp.bfloat16), "ctx", scatter_dimension=0, tiled=True
        ).astype(jnp.float32),
        lax.psum_scatter(
            grad_qkv.astype(jnp.bfloat16), "ctx", scatter_dimension=1, tiled=True
        ).astype(jnp.float32),
        lax.psum_scatter(
            grad_bqv.astype(jnp.bfloat16), "ctx", scatter_dimension=1, tiled=True
        ).astype(jnp.float32),
        lax.psum_scatter(
            grad_wout.astype(jnp.bfloat16), "ctx", scatter_dimension=1, tiled=True
        ).astype(jnp.float32),
        lax.psum_scatter(
            grad_bout.astype(jnp.bfloat16), "ctx", scatter_dimension=0, tiled=True
        ).astype(jnp.float32),
        lax.psum_scatter(
            grad_gain_two.astype(jnp.bfloat16), "ctx", scatter_dimension=0, tiled=True
        ).astype(jnp.float32),
        lax.psum_scatter(
            grad_bias_two.astype(jnp.bfloat16), "ctx", scatter_dimension=0, tiled=True
        ).astype(jnp.float32),
        lax.psum_scatter(
            grad_up.astype(jnp.bfloat16), "ctx", scatter_dimension=0, tiled=True
        ).astype(jnp.float32),
        lax.psum_scatter(
            grad_bup.astype(jnp.bfloat16), "ctx", scatter_dimension=0, tiled=True
        ).astype(jnp.float32),
        lax.psum_scatter(
            grad_down.astype(jnp.bfloat16), "ctx", scatter_dimension=1, tiled=True
        ).astype(jnp.float32),
        lax.psum_scatter(
            grad_bdown.astype(jnp.bfloat16), "ctx", scatter_dimension=0, tiled=True
        ).astype(jnp.float32),
    )
    return (output.astype(jnp.bfloat16), input_grad) + tuple(reduced)


def swap_halves(first, second):
    lane = lax.broadcasted_iota(jnp.int32, first.shape, 1)
    low = lane < HALF
    return (
        jnp.where(low, first, pltpu.roll(second, HALF, 1)),
        jnp.where(low, pltpu.roll(first, HALF, 1), second),
    )


def unpack_pair(ref, index, first_row, count):
    one = ref[index, first_row : first_row + count, :].astype(jnp.float32)
    two = ref[index + 1, first_row : first_row + count, :].astype(jnp.float32)
    return jnp.concatenate(swap_halves(one, two), axis=0)


def pack_pair(ref, index, first_row, count, rows):
    one, two = swap_halves(rows[:count], rows[count:])
    ref[index, first_row : first_row + count, :] = one.astype(ref.dtype)
    ref[index + 1, first_row : first_row + count, :] = two.astype(ref.dtype)


def both_halves(ref, first_row, count):
    return jnp.concatenate(
        [ref[0, first_row : first_row + count, :], ref[1, first_row : first_row + count, :]],
        axis=1,
    )


def dot_of(left, right, left_dim, right_dim):
    return lax.dot_general(
        left, right, (((left_dim,), (right_dim,)), ((), ())), preferred_element_type=jnp.float32
    )


def qkv_kernel(rank_ref, x_ref, gain_ref, bias_ref, w_ref, b_ref, seg_ref, send_ref, own_ref, h_ref):
    step = pl.program_id(0)
    rows = own_ref.shape[0]
    width = own_ref.shape[1]
    heads = width // HDIM

    @pl.when(step == 0)
    def _():
        normed, _ = norm_stats(both_halves(x_ref, 0, rows).astype(jnp.float32))
        h_ref[...] = (normed * gain_ref[...] + bias_ref[...]).astype(jnp.bfloat16)
        own_ref[...] = h_ref[:, pl.ds(pl.multiple_of(rank_ref[0] * width, width), width)]

    flat = jnp.dot(h_ref[...], w_ref[0], preferred_element_type=jnp.float32) + b_ref[0]
    turned = flat.T

    @pl.when(step == 0)
    def _():
        scaled = turned.astype(jnp.bfloat16).astype(jnp.float32) * (1.0 / math.sqrt(HDIM))
        seg_rows = jnp.broadcast_to(seg_ref[...].astype(jnp.float32), (16, rows)).astype(
            jnp.bfloat16
        )
        for head in range(heads):
            pack_pair(send_ref, 2 * head, 2 * HDIM, HDIM // 2, scaled[head * HDIM : (head + 1) * HDIM])
            send_ref[2 * head, SEG_ROW : SEG_ROW + 16, :] = seg_rows
            send_ref[2 * head + 1, SEG_ROW : SEG_ROW + 16, :] = seg_rows

    for which in (1, 2):

        @pl.when(step == which)
        def _(which=which):
            low = turned.astype(jnp.bfloat16)
            for head in range(heads):
                piece = low[head * HDIM : (head + 1) * HDIM]
                send_ref[2 * head, (which - 1) * HDIM : which * HDIM, :] = piece
                send_ref[2 * head + 1, (which - 1) * HDIM : which * HDIM, :] = piece


def masked_scores(keys, query, slope, query_pos, begin, first_key, top):
    score = dot_of(keys, query, 1, 0)
    key_pos = first_key + lax.broadcasted_iota(jnp.int32, score.shape, 0)
    score = score + slope * (key_pos - top).astype(jnp.float32)
    allowed = (key_pos <= query_pos) & (key_pos >= begin)
    return jnp.where(allowed, score, mask_fill)


def doc_starts(recv_ref):
    seg = recv_ref[:, SEG_ROW : SEG_ROW + 16, :].astype(jnp.float32)[:, 0, :]
    one = jnp.sum(jnp.where(seg < 0.5, 1.0, 0.0))
    two = jnp.sum(jnp.where(seg < 1.5, 1.0, 0.0))
    return one.astype(jnp.int32), two.astype(jnp.int32)


def query_geometry(tile, place, starts):
    lane = lax.broadcasted_iota(jnp.int32, (1, QUERIES), 1)
    query_pos = 2 * HALF * (tile * SOURCES + lane // HALF) + HALF * place + lane % HALF
    begin_one, begin_two = starts
    begin = jnp.where(
        query_pos >= begin_two, begin_two, jnp.where(query_pos >= begin_one, begin_one, 0)
    )
    return query_pos, begin


def tile_rows(ref, tile, first_row):
    return jnp.concatenate(
        [
            unpack_pair(ref, tile * SOURCES + pair, first_row, HDIM // 2)
            for pair in range(0, SOURCES, 2)
        ],
        axis=1,
    )


def forward_kernel(slope_ref, place_ref, recv_ref, send_ref, out_ref, lse_ref, key_ref):
    count = recv_ref.shape[0]
    block = 2 * HALF
    slope, place = slope_ref[0], place_ref[0]
    starts = doc_starts(recv_ref)
    for source in range(count):
        key_ref[source * block : (source + 1) * block, :] = (
            recv_ref[source, 0:HDIM, :].astype(jnp.float32).T.astype(jnp.bfloat16)
        )
    values = jnp.concatenate([recv_ref[s, HDIM : 2 * HDIM, :] for s in range(count)], axis=1)
    for tile in range(count // SOURCES):
        reach = (tile + 1) * SOURCES * block
        query = tile_rows(recv_ref, tile, 2 * HDIM).astype(jnp.bfloat16)
        query_pos, begin = query_geometry(tile, place, starts)
        score = masked_scores(key_ref[0:reach, :], query, slope, query_pos, begin, 0, reach)
        high = jnp.max(score, axis=0, keepdims=True)
        weights = jnp.exp(score - high)
        total = jnp.sum(weights, axis=0, keepdims=True)
        out = dot_of(values[:, 0:reach], weights.astype(jnp.bfloat16), 1, 0) / total
        here = slice(tile * QUERIES, (tile + 1) * QUERIES)
        out_ref[:, here] = out
        lse_ref[:, here] = high + jnp.log(total)
        for pair in range(0, SOURCES, 2):
            pack_pair(
                send_ref,
                tile * SOURCES + pair,
                0,
                HDIM // 2,
                out[:, pair * HALF : (pair + 2) * HALF],
            )


def heads_of(ref, first_row):
    return jnp.concatenate(
        [unpack_pair(ref, index, first_row, HDIM // 2) for index in range(0, ref.shape[0], 2)],
        axis=0,
    )


def out_kernel(rank_ref, recv_ref, w_ref, b_ref, part_ref, attn_ref, acc_ref):
    width = w_ref.shape[0]
    turned = heads_of(recv_ref, 0).astype(jnp.bfloat16)
    attn_ref[...] = turned
    acc_ref[...] = dot_of(turned, w_ref[...], 0, 0)
    own = pl.ds(pl.multiple_of(rank_ref[0] * width, width), width)
    acc_ref[:, own] = acc_ref[:, own] + b_ref[...]
    part_ref[...] = acc_ref[...].astype(jnp.bfloat16)


def gelu_pair(value):
    inner = GELU_A * (value + GELU_B * (value * value * value))
    tanh = jnp.tanh(inner)
    half = 0.5 * (1.0 + tanh)
    slope = half + 0.5 * value * (1.0 - tanh * tanh) * (
        GELU_A * (1.0 + 3.0 * GELU_B * (value * value))
    )
    return value * half, slope


def mlp_kernel(
    rank_ref,
    x_ref,
    own_ref,
    other_ref,
    gain_ref,
    bias_ref,
    up_ref,
    b_up_ref,
    down_ref,
    middle_ref,
    hidden_ref,
    act_ref,
    back_ref,
    b_grad_ref,
    share_ref,
    swap_ref,
    grad_acc,
    mlp_acc,
):
    step = pl.program_id(0)
    rows = act_ref.shape[0]
    width = share_ref.shape[1]

    @pl.when(step == 0)
    def _():
        middle = (
            both_halves(x_ref, 0, rows).astype(jnp.float32)
            + own_ref[...].astype(jnp.float32)
            + other_ref[...].astype(jnp.float32)
        )
        middle_ref[...] = middle
        normed, _ = norm_stats(middle.astype(jnp.bfloat16).astype(jnp.float32))
        hidden_ref[...] = (normed * gain_ref[...] + bias_ref[...]).astype(jnp.bfloat16)
        grad_acc[...] = jnp.zeros_like(grad_acc)
        mlp_acc[...] = jnp.zeros_like(mlp_acc)

    pre = jnp.dot(hidden_ref[...], up_ref[...], preferred_element_type=jnp.float32) + b_up_ref[...]
    act, slope = gelu_pair(pre)
    act = act.astype(jnp.bfloat16)
    act_ref[...] = act
    grad_act = dot_of(both_halves(x_ref, rows, rows), down_ref[...], 1, 1)
    grad_pre = (grad_act * slope).astype(jnp.bfloat16)
    back_ref[...] = grad_pre
    b_grad_ref[...] = jnp.sum(grad_pre.astype(jnp.float32), axis=0, keepdims=True)
    grad_acc[...] += dot_of(grad_pre, up_ref[...], 1, 1)
    mlp_acc[...] += jnp.dot(act, down_ref[...], preferred_element_type=jnp.float32)

    @pl.when(step == pl.num_programs(0) - 1)
    def _():
        rank = rank_ref[0]
        swap_ref[:, 0 : 2 * width] = grad_acc[...].astype(jnp.bfloat16)
        swap_ref[:, 2 * width :] = mlp_acc[
            :, pl.ds(pl.multiple_of((1 - rank) * width, width), width)
        ].astype(jnp.bfloat16)
        share_ref[...] = mlp_acc[:, pl.ds(pl.multiple_of(rank * width, width), width)]


def norm_back(whole, normed, inverse, gain):
    scaled = whole * gain
    mean_one = jnp.mean(scaled, axis=-1, keepdims=True)
    mean_two = jnp.mean(scaled * normed, axis=-1, keepdims=True)
    return inverse * (scaled - mean_one - normed * mean_two)


def middle_kernel(
    rank_ref,
    x_ref,
    own_ref,
    other_ref,
    middle_ref,
    share_ref,
    gain_ref,
    b_down_ref,
    w_out_ref,
    mixed_ref,
    grad_ref,
    low_ref,
    send_ref,
    small_ref,
    wide_ref,
):
    rows, width = mixed_ref.shape
    own = pl.ds(pl.multiple_of(rank_ref[0] * width, width), width)
    mixed_ref[...] = (
        middle_ref[:, own]
        + share_ref[...]
        + other_ref[:, 2 * width :].astype(jnp.float32)
        + b_down_ref[...]
    ).astype(jnp.bfloat16)
    whole = own_ref[:, 0 : 2 * width].astype(jnp.float32) + other_ref[:, 0 : 2 * width].astype(
        jnp.float32
    )
    normed, inverse = norm_stats(middle_ref[...].astype(jnp.bfloat16).astype(jnp.float32))
    cot = both_halves(x_ref, rows, rows).astype(jnp.float32)
    grad = cot + norm_back(whole, normed, inverse, gain_ref[...])
    low = grad.astype(jnp.bfloat16)
    low_ref[...] = low
    wide_ref[0:1] = jnp.sum(whole * normed, axis=0, keepdims=True)
    wide_ref[1:2] = jnp.sum(whole, axis=0, keepdims=True)
    wide_ref[2:3] = jnp.sum(grad, axis=0, keepdims=True)
    wide_ref[3:4] = jnp.sum(cot, axis=0, keepdims=True)
    wide_ref[8:, :] = grad
    small_ref[...] = wide_ref[0:8, own]
    grad_ref[...] = wide_ref[8:, own]
    back = dot_of(w_out_ref[...], low, 1, 1).astype(jnp.bfloat16).astype(jnp.float32)
    for head in range(width // HDIM):
        pack_pair(send_ref, 2 * head, 0, HDIM // 2, back[head * HDIM : (head + 1) * HDIM])


def backward_kernel(
    slope_ref,
    place_ref,
    rank_ref,
    recv_ref,
    grad_ref,
    out_ref,
    lse_ref,
    own_ref,
    other_ref,
    send_ref,
    key_ref,
    value_ref,
    key_acc,
    value_acc,
    all_ref,
    weight_ref,
):
    count = recv_ref.shape[0]
    block = 2 * HALF
    slope, place, rank = slope_ref[0], place_ref[0], rank_ref[0]
    starts = doc_starts(recv_ref)
    for source in range(count):
        there = slice(source * block, (source + 1) * block)
        key_ref[there, :] = recv_ref[source, 0:HDIM, :].astype(jnp.float32).T.astype(jnp.bfloat16)
        value_ref[there, :] = (
            recv_ref[source, HDIM : 2 * HDIM, :].astype(jnp.float32).T.astype(jnp.bfloat16)
        )
    keys_turned = jnp.concatenate([recv_ref[s, 0:HDIM, :] for s in range(count)], axis=1)
    key_acc[...] = jnp.zeros_like(key_acc)
    value_acc[...] = jnp.zeros_like(value_acc)
    for tile in range(count // SOURCES):
        reach = (tile + 1) * SOURCES * block
        here = slice(tile * QUERIES, (tile + 1) * QUERIES)
        query = tile_rows(recv_ref, tile, 2 * HDIM).astype(jnp.bfloat16)
        grad_wide = tile_rows(grad_ref, tile, 0)
        grad = grad_wide.astype(jnp.bfloat16)
        delta = jnp.sum(grad_wide * out_ref[:, here], axis=0, keepdims=True)
        query_pos, begin = query_geometry(tile, place, starts)
        score = masked_scores(key_ref[0:reach, :], query, slope, query_pos, begin, 0, reach)
        prob = jnp.exp(score - lse_ref[:, here])
        grad_prob = dot_of(value_ref[0:reach, :], grad, 1, 0)
        grad_score = (prob * (grad_prob - delta)).astype(jnp.bfloat16)
        key_acc[:, 0:reach] += dot_of(query, grad_score, 1, 1)
        value_acc[:, 0:reach] += dot_of(grad, prob.astype(jnp.bfloat16), 1, 1)
        query_grad = dot_of(keys_turned[:, 0:reach], grad_score, 1, 0) * (1.0 / math.sqrt(HDIM))
        query_grad = query_grad.astype(jnp.bfloat16).astype(jnp.float32)
        for pair in range(0, SOURCES, 2):
            index = tile * SOURCES + pair
            piece = query_grad[:, pair * HALF : (pair + 2) * HALF]
            pack_pair(send_ref, index, 2 * HDIM, HDIM // 2, piece)
            other = pltpu.roll(piece, HALF, 1)
            lane = lax.broadcasted_iota(jnp.int32, piece.shape, 1)
            mine = lane // HALF == place
            is_low = place == 0
            all_ref[0:HDIM, index * block : (index + 1) * block] = jnp.where(
                mine, jnp.where(is_low, piece, other), 0.0
            ).astype(jnp.bfloat16)
            all_ref[0:HDIM, (index + 1) * block : (index + 2) * block] = jnp.where(
                mine, jnp.where(is_low, other, piece), 0.0
            ).astype(jnp.bfloat16)
    all_ref[HDIM : 2 * HDIM, :] = key_acc[...].astype(jnp.bfloat16)
    all_ref[2 * HDIM :, :] = value_acc[...].astype(jnp.bfloat16)
    for source in range(count):
        there = slice(source * block, (source + 1) * block)
        send_ref[source, 0 : 2 * HDIM, :] = all_ref[HDIM:, there]
    width = own_ref.shape[1]
    weight_ref[:, pl.ds(pl.multiple_of(rank * width, width), width)] = jnp.dot(
        all_ref[...], own_ref[...], preferred_element_type=jnp.float32
    )
    weight_ref[:, pl.ds(pl.multiple_of((1 - rank) * width, width), width)] = jnp.dot(
        all_ref[...], other_ref[...], preferred_element_type=jnp.float32
    )
    for index in range(0, count, 2):
        pack_pair(
            send_ref,
            index,
            SEG_ROW,
            3 * HDIM // 2,
            weight_ref[:, index * HALF : (index + 2) * HALF],
        )


def hidden_kernel(recv_ref, w_ref, part_ref, weight_ref, b_ref, acc_ref):
    step = pl.program_id(0)
    count = recv_ref.shape[0]

    @pl.when(step == 0)
    def _():
        acc_ref[...] = jnp.zeros_like(acc_ref)
        for index in range(0, count, 2):
            weight_ref[index // 2] = recv_ref[index, SEG_ROW:, :].astype(jnp.float32) + recv_ref[
                index + 1, SEG_ROW:, :
            ].astype(jnp.float32)

    def add(turned):
        acc_ref[...] += dot_of(turned, w_ref[0], 0, 1)
        ones = jnp.ones((8, turned.shape[1]), jnp.bfloat16)
        b_ref[0] = dot_of(ones, turned, 1, 1)

    @pl.when(step == 0)
    def _():
        add(heads_of(recv_ref, 2 * HDIM).astype(jnp.bfloat16))

    for which in (1, 2):

        @pl.when(step == which)
        def _(which=which):
            span = slice((which - 1) * HDIM, which * HDIM)
            add(
                jnp.concatenate(
                    [
                        recv_ref[index, span, :].astype(jnp.float32)
                        + recv_ref[index + 1, span, :].astype(jnp.float32)
                        for index in range(0, count, 2)
                    ],
                    axis=0,
                ).astype(jnp.bfloat16)
            )

    @pl.when(step == 2)
    def _():
        part_ref[...] = acc_ref[...].astype(jnp.bfloat16)


def input_kernel(rank_ref, x_ref, own_ref, other_ref, gain_ref, grad_ref, out_ref, small_ref, wide_ref):
    rows, width = out_ref.shape
    own = pl.ds(pl.multiple_of(rank_ref[0] * width, width), width)
    normed, inverse = norm_stats(both_halves(x_ref, 0, rows).astype(jnp.float32))
    whole = own_ref[...].astype(jnp.float32) + other_ref[...].astype(jnp.float32)
    wide_ref[0:1] = jnp.sum(whole * normed, axis=0, keepdims=True)
    wide_ref[1:2] = jnp.sum(whole, axis=0, keepdims=True)
    wide_ref[8:, :] = norm_back(whole, normed, inverse, gain_ref[...])
    small_ref[...] = wide_ref[0:8, own]
    out_ref[...] = (grad_ref[...] + wide_ref[8:, own]).astype(jnp.bfloat16)


def call(kernel, outs, ins, scratch=(), grid=None, in_specs=None, out_specs=None, cost=None):
    vmem = pl.BlockSpec(memory_space=pltpu.VMEM)
    smem = pl.BlockSpec(memory_space=pltpu.SMEM)
    specs = in_specs or [smem if value.ndim == 1 else vmem for value in ins]
    options = {} if grid is None else {"grid": grid}
    return pl.pallas_call(
        kernel,
        out_shape=[jax.ShapeDtypeStruct(shape, dtype) for shape, dtype in outs],
        in_specs=specs,
        out_specs=out_specs or [vmem] * len(outs),
        scratch_shapes=list(scratch),
        compiler_params=pltpu.CompilerParams(vmem_limit_bytes=48 * 1024 * 1024),
        cost_estimate=pl.CostEstimate(
            flops=cost or 10**8, bytes_accessed=4 * 10**6, transcendentals=0
        ),
        **options,
    )(*ins)


def stripes(left, ctx_bits, axis_bits, chosen, value):
    dims = (left.shape[0],) + (2,) * len(ctx_bits) + (-1,)
    spread = left.reshape(dims)
    at = 1 + ctx_bits.index(chosen)
    kept = lax.dynamic_index_in_dim(spread, value, at, keepdims=False)
    rest = [bit for bit in ctx_bits if bit != chosen]
    order = [0] + [1 + rest.index(bit) for bit in axis_bits] + [1 + len(rest)]
    return jnp.transpose(kept, order).reshape(left.shape[0], -1)


def swap_over(value, bit, count):
    return lax.ppermute(value, "ctx", [(place, place ^ (1 << bit)) for place in range(count)])


def reduce_rows(left, right, right_dim, place, count, order, gather):
    bits = tuple(reversed(range(count.bit_length() - 1)))
    bit_of = lambda bit: (place >> bit) & 1
    if gather:
        first, order = order[0], order[1:]
        mine = stripes(left, bits, order, first, bit_of(first))
        theirs = stripes(left, bits, order, first, 1 - bit_of(first))
        left = jnp.concatenate([mine, swap_over(theirs, first, count)], axis=0)
        right = jnp.concatenate([right, swap_over(right, first, count)], axis=0)
        bits = order
    first, order = order[0], order[1:]
    send = dot_of(
        stripes(left, bits, order, first, 1 - bit_of(first)), right, 0, right_dim
    ).astype(jnp.bfloat16)
    keep = dot_of(stripes(left, bits, order, first, bit_of(first)), right, 0, right_dim)
    total = keep + swap_over(send, first, count).astype(jnp.float32)
    for bit in order:
        half = total.shape[0] // 2
        send = lax.dynamic_slice_in_dim(total, (1 - bit_of(bit)) * half, half, 0)
        keep = lax.dynamic_slice_in_dim(total, bit_of(bit) * half, half, 0)
        total = keep + swap_over(send.astype(jnp.bfloat16), bit, count).astype(jnp.float32)
    return total


def on_device_paired(
    tokens,
    segment_ids,
    ln1_gain,
    ln1_bias,
    w_qkv,
    b_qv,
    w_out,
    b_out,
    ln2_gain,
    ln2_bias,
    w_up,
    b_up,
    w_down,
    b_down,
    cotangent,
    count,
):
    bf16, f32 = jnp.bfloat16, jnp.float32
    rows, width = tokens.shape
    model = w_out.shape[1]
    hidden = w_up.shape[1]
    heads = width // HDIM
    block = 2 * HALF
    all_tokens = count * rows
    tp_rank = lax.axis_index("tp")
    place = lax.axis_index("ctx")
    rank = tp_rank.reshape(1)
    side = (place % 2).reshape(1)
    slope = head_slopes(tp_rank * heads + place // 2, 1)
    gain_one, bias_one = ln1_gain.reshape(1, model), ln1_bias.reshape(1, model)
    gain_two, bias_two = ln2_gain.reshape(1, model), ln2_bias.reshape(1, model)
    other_core = lambda value: lax.ppermute(value, "tp", [(0, 1), (1, 0)])
    to_heads = lambda value: lax.all_to_all(value, "ctx", 0, 0, tiled=True)
    smem = pl.BlockSpec(memory_space=pltpu.SMEM)
    whole = lambda *shape: pl.BlockSpec(shape, lambda step: (0,) * len(shape))

    pair_in = lax.all_gather(jnp.concatenate([tokens, cotangent], axis=0), "tp")
    b_three = jnp.stack([b_qv[0], jnp.zeros_like(b_qv[0]), b_qv[1]]).reshape(3, 1, width)
    sent, h_own, _ = call(
        qkv_kernel,
        [((count, FWD_ROWS, rows), bf16), ((rows, width), bf16), ((rows, model), bf16)],
        [rank, pair_in, gain_one, bias_one, w_qkv, b_three, segment_ids.reshape(1, rows)],
        grid=(3,),
        in_specs=[
            smem,
            whole(2, 2 * rows, width),
            whole(1, model),
            whole(1, model),
            pl.BlockSpec((1, model, width), lambda step: (step, 0, 0)),
            pl.BlockSpec((1, 1, width), lambda step: (step, 0, 0)),
            whole(1, rows),
        ],
        out_specs=[whole(count, FWD_ROWS, rows), whole(rows, width), whole(rows, model)],
    )
    h_all_own = lax.all_gather(h_own, "ctx", axis=0, tiled=True)
    h_all_other = other_core(h_all_own)
    got = to_heads(sent)
    attn_sent, attn_raw, lse = call(
        forward_kernel,
        [
            ((count, HDIM // 2, rows), bf16),
            ((HDIM, all_tokens // 2), f32),
            ((1, all_tokens // 2), f32),
        ],
        [slope, side, got],
        scratch=[pltpu.VMEM((all_tokens, HDIM), bf16)],
    )
    attn_got = to_heads(attn_sent)
    part, attn_turned = call(
        out_kernel,
        [((rows, model), bf16), ((width, rows), bf16)],
        [rank, attn_got, w_out, b_out.reshape(1, width)],
        scratch=[pltpu.VMEM((rows, model), f32)],
    )
    chunk = 512
    middle, h_two, act, grad_pre, grad_b_up, share, swap = call(
        mlp_kernel,
        [
            ((rows, model), f32),
            ((rows, model), bf16),
            ((rows, hidden), bf16),
            ((rows, hidden), bf16),
            ((1, hidden), f32),
            ((rows, width), f32),
            ((rows, model + width), bf16),
        ],
        [
            rank,
            pair_in,
            part,
            other_core(part),
            gain_two,
            bias_two,
            w_up,
            b_up.reshape(1, hidden),
            w_down,
        ],
        grid=(hidden // chunk,),
        in_specs=[
            smem,
            whole(2, 2 * rows, width),
            whole(rows, model),
            whole(rows, model),
            whole(1, model),
            whole(1, model),
            pl.BlockSpec((model, chunk), lambda step: (0, step)),
            pl.BlockSpec((1, chunk), lambda step: (0, step)),
            pl.BlockSpec((chunk, model), lambda step: (step, 0)),
        ],
        out_specs=[
            whole(rows, model),
            whole(rows, model),
            pl.BlockSpec((rows, chunk), lambda step: (0, step)),
            pl.BlockSpec((rows, chunk), lambda step: (0, step)),
            pl.BlockSpec((1, chunk), lambda step: (0, step)),
            whole(rows, width),
            whole(rows, model + width),
        ],
        scratch=[pltpu.VMEM((rows, model), f32), pltpu.VMEM((rows, model), f32)],
    )
    mixed, grad_mid, grad_low, grad_sent, small_two = call(
        middle_kernel,
        [
            ((rows, width), bf16),
            ((rows, width), f32),
            ((rows, model), bf16),
            ((count, HDIM // 2, rows), bf16),
            ((8, width), f32),
        ],
        [
            rank,
            pair_in,
            swap,
            other_core(swap),
            middle,
            share,
            gain_two,
            b_down.reshape(1, width),
            w_out,
        ],
        scratch=[pltpu.VMEM((rows + 8, model), f32)],
    )
    cot_full = jnp.concatenate([pair_in[0, rows:], pair_in[1, rows:]], axis=1)
    bit_x, bit_y, bit_z, bit_far = 0, 1, 2, 3
    grad_down = reduce_rows(
        cot_full, act, 0, place, count, (bit_x, bit_y, bit_z, bit_far), True
    )
    grad_up = reduce_rows(
        h_two, grad_pre, 0, place, count, (bit_y, bit_x, bit_z, bit_far), True
    )
    grad_out = reduce_rows(
        grad_low, attn_turned, 1, place, count, (bit_x, bit_y, bit_z, bit_far), False
    )
    (back_sent,) = call(
        backward_kernel,
        [((count, BACK_ROWS, rows), bf16)],
        [slope, side, rank, got, to_heads(grad_sent), attn_raw, lse, h_all_own, h_all_other],
        scratch=[
            pltpu.VMEM((all_tokens, HDIM), bf16),
            pltpu.VMEM((all_tokens, HDIM), bf16),
            pltpu.VMEM((HDIM, all_tokens), f32),
            pltpu.VMEM((HDIM, all_tokens), f32),
            pltpu.VMEM((3 * HDIM, all_tokens), bf16),
            pltpu.VMEM((3 * HDIM, model), f32),
        ],
    )
    back_got = to_heads(back_sent)
    part_one, grad_qkv, sums = call(
        hidden_kernel,
        [
            ((rows, model), bf16),
            ((heads, BACK_ROWS - SEG_ROW, rows), f32),
            ((3, 8, width), f32),
        ],
        [back_got, w_qkv],
        grid=(3,),
        in_specs=[
            whole(count, BACK_ROWS, rows),
            pl.BlockSpec((1, model, width), lambda step: (step, 0, 0)),
        ],
        out_specs=[
            whole(rows, model),
            whole(heads, BACK_ROWS - SEG_ROW, rows),
            pl.BlockSpec((1, 8, width), lambda step: (step, 0, 0)),
        ],
        scratch=[pltpu.VMEM((rows, model), f32)],
    )
    input_grad, small_one = call(
        input_kernel,
        [((rows, width), bf16), ((8, width), f32)],
        [rank, pair_in, part_one, other_core(part_one), gain_one, grad_mid],
        scratch=[pltpu.VMEM((rows + 8, model), f32)],
    )
    share_w = width // count
    vectors = jnp.concatenate(
        [
            small_one[0:2].reshape(2, count, share_w),
            sums[0:3:2, 0].reshape(2, count, share_w),
            small_two[0:4].reshape(4, count, share_w),
            grad_b_up.reshape(count, -1, share_w).transpose(1, 0, 2),
        ],
        axis=0,
    )
    lanes = vectors.shape[0] * share_w
    spread = vectors.transpose(1, 0, 2).reshape(count, 1, lanes)
    total = jnp.sum(to_heads(spread), axis=0).reshape(-1, share_w)
    stripe = model // count
    grad_qkv = (
        grad_qkv.reshape(heads, 3 * HDIM // 2, 2, stripe)
        .transpose(0, 2, 1, 3)
        .reshape(heads, 3, HDIM, stripe)
        .transpose(1, 3, 0, 2)
        .reshape(3, stripe, width)
    )
    return (
        mixed,
        input_grad,
        total[0],
        total[1],
        grad_qkv,
        total[2:4],
        grad_out.T,
        total[6],
        total[4],
        total[5],
        grad_up,
        total[8:].reshape(-1),
        grad_down.T,
        total[7],
    )


def paired(mesh, arrays):
    sizes = dict(mesh.shape)
    count, cores = sizes["ctx"], sizes["tp"]
    rows = arrays[0].shape[0] // count
    return (
        cores == 2
        and count == 16
        and rows == 2 * HALF
        and count * cores == 2 * HEADS
        and arrays[0].shape[1] == HEADS * HDIM
    )


def solution(mesh):
    in_specs = (
        P("ctx", "tp"),
        P("ctx"),
        P(),
        P(),
        P(None, None, "tp"),
        P(None, "tp"),
        P("tp", None),
        P("tp"),
        P(),
        P(),
        P(None, "tp"),
        P("tp"),
        P("tp", None),
        P("tp"),
        P("ctx", "tp"),
    )
    out_specs = (
        P("ctx", "tp"),
        P("ctx", "tp"),
        P(("tp", "ctx")),
        P(("tp", "ctx")),
        P(None, "ctx", "tp"),
        P(None, ("tp", "ctx")),
        P("tp", "ctx"),
        P(("tp", "ctx")),
        P(("tp", "ctx")),
        P(("tp", "ctx")),
        P("ctx", "tp"),
        P(("tp", "ctx")),
        P("tp", "ctx"),
        P(("tp", "ctx")),
    )

    def run(*arrays):
        if paired(mesh, arrays):
            body = functools.partial(on_device_paired, count=dict(mesh.shape)["ctx"])
        else:
            body = on_device
        return jax.shard_map(
            body, mesh=mesh, in_specs=in_specs, out_specs=out_specs, check_vma=False
        )(*arrays)

    return run
```

```python
import functools
import math

import jax
import jax.numpy as jnp
from jax import lax
from jax.experimental import pallas as pl
from jax.experimental.pallas import tpu as pltpu
from jax.sharding import PartitionSpec as P

HEADS = 16
HDIM = 64


norm_eps = 1e-05
mask_fill = -1e30
score_block = 512

HALF = 64
SOURCES = 4
QUERIES = SOURCES * HALF
SEG_ROW = 5 * HDIM // 2
FWD_ROWS = SEG_ROW + 16
GELU_A = math.sqrt(2.0 / math.pi)
GELU_B = 0.044715

DOWN_BITS = (0, 1, 2, 3)
UP_BITS = (2, 0, 1, 3)
GATHERED = (0, 8, 4, 12, 1, 9, 5, 13, 2, 10, 6, 14, 3, 11, 7, 15)


def head_slopes(first_head, head_count):
    index_list = first_head + jnp.arange(head_count, dtype=jnp.int32)
    return jnp.exp2(-8.0 * (index_list + 1).astype(jnp.float32) / HEADS)


def pair_scores(query_heads, query_pos, query_seg, key_heads, key_pos, key_seg, slopes):
    logits = jnp.einsum(
        "qhd,khd->hqk", query_heads, key_heads, preferred_element_type=jnp.float32
    ) / math.sqrt(HDIM)
    distance = (key_pos[None, :] - query_pos[:, None]).astype(jnp.float32)
    allowed = (key_pos[None, :] <= query_pos[:, None]) & (key_seg[None, :] == query_seg[:, None])
    return (
        jnp.where(allowed[None], logits + slopes[:, None, None] * distance[None], mask_fill),
        allowed,
    )


def block_grads(
    query_heads,
    query_pos,
    query_seg,
    grad_heads,
    lse_rows,
    delta_rows,
    key_heads,
    value_heads,
    key_pos,
    key_seg,
    slopes,
):
    score, allowed = pair_scores(
        query_heads, query_pos, query_seg, key_heads, key_pos, key_seg, slopes
    )
    prob = jnp.where(allowed[None], jnp.exp(score - lse_rows.T[:, :, None]), 0.0)
    grad_prob = jnp.einsum(
        "qhd,khd->hqk", grad_heads, value_heads, preferred_element_type=jnp.float32
    )
    grad_score = (prob * (grad_prob - delta_rows.T[:, :, None])).astype(jnp.bfloat16)
    return (prob.astype(jnp.bfloat16), grad_score)


def over_blocks(row_count, step_fn, state_now):
    return lax.fori_loop(
        0,
        row_count // score_block,
        lambda number, inner_state: step_fn(number * score_block, score_block, inner_state),
        state_now,
    )


def seg_at(seg_array, where_row):
    return lax.dynamic_slice_in_dim(seg_array, where_row, 1)[0]


def gather_features(local_rows):
    return lax.all_gather(local_rows, "tp", axis=1, tiled=True)


def norm_stats(full_rows):
    center = full_rows - jnp.mean(full_rows, axis=-1, keepdims=True)
    inverse = lax.rsqrt(jnp.mean(center * center, axis=-1, keepdims=True) + norm_eps)
    return (center * inverse, inverse)


def norm_backward(part_grad, normed, inverse, gain, tp_rank, local_width):
    offset = tp_rank * local_width
    whole_grad = lax.psum(part_grad.astype(jnp.bfloat16), "tp").astype(jnp.float32)
    scaled = whole_grad * gain
    mean_one = jnp.mean(scaled, axis=-1, keepdims=True)
    mean_two = jnp.mean(scaled * normed, axis=-1, keepdims=True)
    input_grad = lax.dynamic_slice_in_dim(
        inverse * (scaled - mean_one - normed * mean_two), offset, local_width, 1
    )
    share_grad = lax.dynamic_slice_in_dim(whole_grad, offset, local_width, 1)
    normed_share = lax.dynamic_slice_in_dim(normed, offset, local_width, 1)
    gain_grad = jnp.sum(share_grad * normed_share, axis=0)
    bias_grad = jnp.sum(share_grad, axis=0)
    return (input_grad, gain_grad, bias_grad)


def on_device(
    tokens,
    segment_ids,
    ln1_gain,
    ln1_bias,
    w_qkv,
    b_qv,
    w_out,
    b_out,
    ln2_gain,
    ln2_bias,
    w_up,
    b_up,
    w_down,
    b_down,
    cotangent,
):
    local_rows, local_width = tokens.shape
    heads_local = local_width // HDIM
    tp_rank = lax.axis_index("tp")
    ctx_rank = lax.axis_index("ctx")
    slopes = head_slopes(tp_rank * heads_local, heads_local)
    own_pos = ctx_rank * local_rows + jnp.arange(local_rows, dtype=jnp.int32)
    own_first_seg = segment_ids[0]
    own_last_seg = segment_ids[-1]
    full_in = gather_features(tokens)
    normed_one, inverse_one = norm_stats(full_in.astype(jnp.float32))
    hidden_one = (normed_one * ln1_gain + ln1_bias).astype(jnp.bfloat16)
    projected = jnp.einsum("td,cde->cte", hidden_one, w_qkv, preferred_element_type=jnp.float32)
    query_rows = (projected[0] + b_qv[0]).astype(jnp.bfloat16)
    key_rows = projected[1].astype(jnp.bfloat16)
    value_rows = (projected[2] + b_qv[1]).astype(jnp.bfloat16)
    query_heads = query_rows.reshape(local_rows, heads_local, HDIM)
    key_heads = key_rows.reshape(local_rows, heads_local, HDIM)
    value_heads = value_rows.reshape(local_rows, heads_local, HDIM)
    start_state = (
        jnp.full((heads_local, local_rows), mask_fill, jnp.float32),
        jnp.zeros((heads_local, local_rows), jnp.float32),
        jnp.zeros((heads_local, local_rows, HDIM), jnp.float32),
    )
    piece_keys = lax.all_gather(key_rows, "ctx", axis=0, tiled=True)
    piece_values = lax.all_gather(value_rows, "ctx", axis=0, tiled=True)
    piece_seg = lax.all_gather(segment_ids, "ctx", axis=0, tiled=True)

    def forward_one_block(offset, size_each, inner_state):

        def attend(running):
            high_now, total_now, acc_now = running
            block_keys = lax.dynamic_slice_in_dim(piece_keys, offset, size_each).reshape(
                size_each, heads_local, HDIM
            )
            block_values = lax.dynamic_slice_in_dim(piece_values, offset, size_each).reshape(
                size_each, heads_local, HDIM
            )
            block_seg = lax.dynamic_slice_in_dim(piece_seg, offset, size_each)
            key_pos = offset + jnp.arange(size_each, dtype=jnp.int32)
            score, allowed = pair_scores(
                query_heads, own_pos, segment_ids, block_keys, key_pos, block_seg, slopes
            )
            high_new = jnp.maximum(high_now, jnp.max(score, axis=-1))
            weights = jnp.where(allowed[None], jnp.exp(score - high_new[:, :, None]), 0.0)
            factor = jnp.exp(high_now - high_new)
            total_new = total_now * factor + jnp.sum(weights, axis=-1)
            acc_new = acc_now * factor[:, :, None] + jnp.einsum(
                "hqk,khd->hqd",
                weights.astype(jnp.bfloat16),
                block_values,
                preferred_element_type=jnp.float32,
            )
            return (high_new, total_new, acc_new)

        needed = (offset <= own_pos[-1]) & (
            seg_at(piece_seg, offset + size_each - 1) >= own_first_seg
        )
        return lax.cond(needed, attend, lambda running: running, inner_state)

    high_fin, total_fin, acc_fin = over_blocks(piece_keys.shape[0], forward_one_block, start_state)
    attn_raw = jnp.transpose(acc_fin / total_fin[:, :, None], (1, 0, 2)).reshape(
        local_rows, local_width
    )
    lse_rows = (high_fin + jnp.log(total_fin)).T
    attn_low = attn_raw.astype(jnp.bfloat16)
    attn_share = lax.psum_scatter(
        jnp.dot(attn_low, w_out, preferred_element_type=jnp.float32).astype(jnp.bfloat16),
        "tp",
        scatter_dimension=1,
        tiled=True,
    ).astype(jnp.float32)
    middle = tokens.astype(jnp.float32) + attn_share + b_out
    full_mid = gather_features(middle.astype(jnp.bfloat16))
    normed_two, inverse_two = norm_stats(full_mid.astype(jnp.float32))
    hidden_two = (normed_two * ln2_gain + ln2_bias).astype(jnp.bfloat16)
    pre_act = jnp.dot(hidden_two, w_up, preferred_element_type=jnp.float32) + b_up
    gelu_out, gelu_back = jax.vjp(
        lambda pre_value: jax.nn.gelu(pre_value, approximate=True), pre_act
    )
    activated = gelu_out.astype(jnp.bfloat16)
    mlp_share = lax.psum_scatter(
        jnp.dot(activated, w_down, preferred_element_type=jnp.float32).astype(jnp.bfloat16),
        "tp",
        scatter_dimension=1,
        tiled=True,
    ).astype(jnp.float32)
    output = middle + mlp_share + b_down
    contract_rows = (((0,), (0,)), ((), ()))
    contract_cols = (((1,), (1,)), ((), ()))
    out_grad = cotangent.astype(jnp.float32)
    full_cot = gather_features(cotangent)
    grad_down = lax.dot_general(
        activated, full_cot, contract_rows, preferred_element_type=jnp.float32
    )
    grad_act = lax.dot_general(full_cot, w_down, contract_cols, preferred_element_type=jnp.float32)
    grad_pre = gelu_back(grad_act)[0].astype(jnp.bfloat16)
    grad_bup = jnp.sum(grad_pre.astype(jnp.float32), axis=0)
    grad_up = lax.dot_general(
        hidden_two, grad_pre, contract_rows, preferred_element_type=jnp.float32
    )
    part_two = lax.dot_general(grad_pre, w_up, contract_cols, preferred_element_type=jnp.float32)
    grad_mid_norm, grad_gain_two, grad_bias_two = norm_backward(
        part_two, normed_two, inverse_two, ln2_gain, tp_rank, local_width
    )
    grad_middle = out_grad + grad_mid_norm
    grad_bdown = jnp.sum(out_grad, axis=0)
    grad_bout = jnp.sum(grad_middle, axis=0)
    full_back = gather_features(grad_middle.astype(jnp.bfloat16))
    grad_wout = lax.dot_general(
        attn_low, full_back, contract_rows, preferred_element_type=jnp.float32
    )
    grad_attn = lax.dot_general(
        full_back, w_out, contract_cols, preferred_element_type=jnp.float32
    ).astype(jnp.bfloat16)
    grad_heads = grad_attn.reshape(local_rows, heads_local, HDIM)
    delta_rows = jnp.sum(
        grad_heads.astype(jnp.float32) * attn_raw.reshape(local_rows, heads_local, HDIM), axis=-1
    )
    query_zero = jnp.zeros((local_rows, heads_local, HDIM), jnp.float32)
    back_state = (query_zero,)
    backward_piece_keys = lax.all_gather(key_rows, "ctx", axis=0, tiled=True)
    backward_piece_values = lax.all_gather(value_rows, "ctx", axis=0, tiled=True)
    backward_piece_seg = lax.all_gather(segment_ids, "ctx", axis=0, tiled=True)

    def backward_one_block(offset, size_each, inner_state):

        def backward_work(running):
            block_keys = lax.dynamic_slice_in_dim(backward_piece_keys, offset, size_each).reshape(
                size_each, heads_local, HDIM
            )
            block_values = lax.dynamic_slice_in_dim(
                backward_piece_values, offset, size_each
            ).reshape(size_each, heads_local, HDIM)
            block_seg = lax.dynamic_slice_in_dim(backward_piece_seg, offset, size_each)
            key_pos = offset + jnp.arange(size_each, dtype=jnp.int32)
            prob_low, grad_score = block_grads(
                query_heads,
                own_pos,
                segment_ids,
                grad_heads,
                lse_rows,
                delta_rows,
                block_keys,
                block_values,
                key_pos,
                block_seg,
                slopes,
            )
            query_acc = running[0] + jnp.einsum(
                "hqk,khd->qhd", grad_score, block_keys, preferred_element_type=jnp.float32
            ) / math.sqrt(HDIM)
            return (query_acc,)

        needed = (offset <= own_pos[-1]) & (
            seg_at(backward_piece_seg, offset + size_each - 1) >= own_first_seg
        )
        return lax.cond(needed, backward_work, lambda running: running, inner_state)

    back_result = over_blocks(backward_piece_keys.shape[0], backward_one_block, back_state)
    query_grad = back_result[0].reshape(local_rows, local_width)
    piece_query = lax.all_gather(query_rows, "ctx", axis=0, tiled=True)
    piece_grad = lax.all_gather(grad_attn, "ctx", axis=0, tiled=True)
    piece_lse = lax.all_gather(lse_rows.astype(jnp.bfloat16), "ctx", axis=0, tiled=True).astype(
        jnp.float32
    )
    piece_delta = lax.all_gather(delta_rows.astype(jnp.bfloat16), "ctx", axis=0, tiled=True).astype(
        jnp.float32
    )
    owner_piece_seg = lax.all_gather(segment_ids, "ctx", axis=0, tiled=True)

    def owner_one_block(offset, size_each, inner_state):

        def owner_work(running):
            key_acc, value_acc = running
            block_query = lax.dynamic_slice_in_dim(piece_query, offset, size_each).reshape(
                size_each, heads_local, HDIM
            )
            block_grad = lax.dynamic_slice_in_dim(piece_grad, offset, size_each).reshape(
                size_each, heads_local, HDIM
            )
            block_lse = lax.dynamic_slice_in_dim(piece_lse, offset, size_each)
            block_delta = lax.dynamic_slice_in_dim(piece_delta, offset, size_each)
            block_seg = lax.dynamic_slice_in_dim(owner_piece_seg, offset, size_each)
            query_pos = offset + jnp.arange(size_each, dtype=jnp.int32)
            prob_low, grad_score = block_grads(
                block_query,
                query_pos,
                block_seg,
                block_grad,
                block_lse,
                block_delta,
                key_heads,
                value_heads,
                own_pos,
                segment_ids,
                slopes,
            )
            key_acc = key_acc + jnp.einsum(
                "hqk,qhd->khd", grad_score, block_query, preferred_element_type=jnp.float32
            ) / math.sqrt(HDIM)
            value_acc = value_acc + jnp.einsum(
                "hqk,qhd->khd", prob_low, block_grad, preferred_element_type=jnp.float32
            )
            return (key_acc, value_acc)

        needed = (offset + size_each - 1 >= own_pos[0]) & (
            seg_at(owner_piece_seg, offset) <= own_last_seg
        )
        return lax.cond(needed, owner_work, lambda running: running, inner_state)

    key_acc, value_acc = over_blocks(
        piece_query.shape[0], owner_one_block, (query_zero, query_zero)
    )
    key_grad = key_acc.reshape(local_rows, local_width)
    value_grad = value_acc.reshape(local_rows, local_width)
    query_low = query_grad.astype(jnp.bfloat16)
    key_low = key_grad.astype(jnp.bfloat16)
    value_low = value_grad.astype(jnp.bfloat16)
    grad_bqv = jnp.stack(
        (
            jnp.sum(query_low.astype(jnp.float32), axis=0),
            jnp.sum(value_low.astype(jnp.float32), axis=0),
        )
    )
    stacked_grads = jnp.stack((query_low, key_low, value_low))
    grad_qkv = jnp.einsum(
        "td,cte->cde", hidden_one, stacked_grads, preferred_element_type=jnp.float32
    )
    part_one = jnp.einsum("cte,cde->td", stacked_grads, w_qkv, preferred_element_type=jnp.float32)
    grad_in_norm, grad_gain_one, grad_bias_one = norm_backward(
        part_one, normed_one, inverse_one, ln1_gain, tp_rank, local_width
    )
    input_grad = (grad_middle + grad_in_norm).astype(jnp.bfloat16)
    reduced = (
        lax.psum_scatter(
            grad_gain_one.astype(jnp.bfloat16), "ctx", scatter_dimension=0, tiled=True
        ).astype(jnp.float32),
        lax.psum_scatter(
            grad_bias_one.astype(jnp.bfloat16), "ctx", scatter_dimension=0, tiled=True
        ).astype(jnp.float32),
        lax.psum_scatter(
            grad_qkv.astype(jnp.bfloat16), "ctx", scatter_dimension=1, tiled=True
        ).astype(jnp.float32),
        lax.psum_scatter(
            grad_bqv.astype(jnp.bfloat16), "ctx", scatter_dimension=1, tiled=True
        ).astype(jnp.float32),
        lax.psum_scatter(
            grad_wout.astype(jnp.bfloat16), "ctx", scatter_dimension=1, tiled=True
        ).astype(jnp.float32),
        lax.psum_scatter(
            grad_bout.astype(jnp.bfloat16), "ctx", scatter_dimension=0, tiled=True
        ).astype(jnp.float32),
        lax.psum_scatter(
            grad_gain_two.astype(jnp.bfloat16), "ctx", scatter_dimension=0, tiled=True
        ).astype(jnp.float32),
        lax.psum_scatter(
            grad_bias_two.astype(jnp.bfloat16), "ctx", scatter_dimension=0, tiled=True
        ).astype(jnp.float32),
        lax.psum_scatter(
            grad_up.astype(jnp.bfloat16), "ctx", scatter_dimension=0, tiled=True
        ).astype(jnp.float32),
        lax.psum_scatter(
            grad_bup.astype(jnp.bfloat16), "ctx", scatter_dimension=0, tiled=True
        ).astype(jnp.float32),
        lax.psum_scatter(
            grad_down.astype(jnp.bfloat16), "ctx", scatter_dimension=1, tiled=True
        ).astype(jnp.float32),
        lax.psum_scatter(
            grad_bdown.astype(jnp.bfloat16), "ctx", scatter_dimension=0, tiled=True
        ).astype(jnp.float32),
    )
    return (output.astype(jnp.bfloat16), input_grad) + tuple(reduced)


def swap_halves(first, second):
    lane = lax.broadcasted_iota(jnp.int32, first.shape, 1)
    low = lane < HALF
    return (
        jnp.where(low, first, pltpu.roll(second, HALF, 1)),
        jnp.where(low, pltpu.roll(first, HALF, 1), second),
    )


def unpack_pair(ref, index, first_row, count):
    one = ref[index, first_row : first_row + count, :].astype(jnp.float32)
    two = ref[index + 1, first_row : first_row + count, :].astype(jnp.float32)
    return jnp.concatenate(swap_halves(one, two), axis=0)


def pack_pair(ref, index, first_row, count, rows):
    one, two = swap_halves(rows[:count], rows[count:])
    ref[index, first_row : first_row + count, :] = one.astype(ref.dtype)
    ref[index + 1, first_row : first_row + count, :] = two.astype(ref.dtype)


def dot_of(left, right, left_dim, right_dim):
    return lax.dot_general(
        left, right, (((left_dim,), (right_dim,)), ((), ())), preferred_element_type=jnp.float32
    )


def put_halves(ref, rank, own_ref, other_ref):
    width = own_ref.shape[1]
    ref[:, pl.ds(pl.multiple_of(rank * width, width), width)] = own_ref[...]
    ref[:, pl.ds(pl.multiple_of((1 - rank) * width, width), width)] = other_ref[...]


def put_stripes(ref, first_lane, turned_ref, chosen, order, value):
    side = 2 * HALF
    for number in range(1 << len(order)):
        source = 0
        for depth, bit in enumerate(order):
            source |= ((number >> (len(order) - 1 - depth)) & 1) << bit
        start = pl.multiple_of((source + (value << chosen)) * HALF, HALF)
        row, lane = (number * HALF) % side, first_lane + (number * HALF) // side * side
        ref[row : row + HALF, lane : lane + side] = turned_ref[pl.ds(start, HALF), :]


def qkv_kernel(
    rank_ref,
    place_ref,
    x_own_ref,
    x_other_ref,
    cot_own_ref,
    cot_other_ref,
    gain_ref,
    bias_ref,
    w_ref,
    b_ref,
    seg_ref,
    send_ref,
    x_ref,
    cot_ref,
    mine_ref,
    theirs_ref,
    h_ref,
    turn_ref,
):
    step = pl.program_id(0)
    rows, width = x_own_ref.shape
    heads = width // HDIM

    @pl.when(step == 0)
    def _():
        put_halves(x_ref, rank_ref[0], x_own_ref, x_other_ref)
        normed, _ = norm_stats(x_ref[...].astype(jnp.float32))
        h_ref[...] = (normed * gain_ref[...] + bias_ref[...]).astype(jnp.bfloat16)

    @pl.when(step == 2)
    def _():
        put_halves(cot_ref, rank_ref[0], cot_own_ref, cot_other_ref)
        turn_ref[...] = cot_ref[...].astype(jnp.float32).T.astype(jnp.bfloat16)
        bit = (place_ref[0] >> DOWN_BITS[0]) & 1
        put_stripes(mine_ref, 0, turn_ref, DOWN_BITS[0], DOWN_BITS[1:], bit)
        put_stripes(theirs_ref, 0, turn_ref, DOWN_BITS[0], DOWN_BITS[1:], 1 - bit)

    bias = jnp.where(step == 0, b_ref[0:1], jnp.where(step == 2, b_ref[1:2], 0.0))
    flat = jnp.dot(h_ref[...], w_ref[0], preferred_element_type=jnp.float32) + bias
    turned = flat.T

    @pl.when(step == 0)
    def _():
        scaled = turned.astype(jnp.bfloat16).astype(jnp.float32) * (1.0 / math.sqrt(HDIM))
        seg_rows = jnp.broadcast_to(seg_ref[...].astype(jnp.float32), (16, rows)).astype(
            jnp.bfloat16
        )
        for head in range(heads):
            pack_pair(send_ref, 2 * head, 2 * HDIM, HDIM // 2, scaled[head * HDIM : (head + 1) * HDIM])
            send_ref[2 * head, SEG_ROW : SEG_ROW + 16, :] = seg_rows
            send_ref[2 * head + 1, SEG_ROW : SEG_ROW + 16, :] = seg_rows

    for which in (1, 2):

        @pl.when(step == which)
        def _(which=which):
            low = turned.astype(jnp.bfloat16)
            for head in range(heads):
                piece = low[head * HDIM : (head + 1) * HDIM]
                send_ref[2 * head, (which - 1) * HDIM : which * HDIM, :] = piece
                send_ref[2 * head + 1, (which - 1) * HDIM : which * HDIM, :] = piece


def masked_scores(keys, query, slope, query_pos, begin, first_key, top):
    score = dot_of(keys, query, 1, 0)
    key_pos = first_key + lax.broadcasted_iota(jnp.int32, score.shape, 0)
    score = score + slope * (key_pos - top).astype(jnp.float32)
    allowed = (key_pos <= query_pos) & (key_pos >= begin)
    return jnp.where(allowed, score, mask_fill)


def doc_starts(recv_ref):
    seg = recv_ref[:, SEG_ROW : SEG_ROW + 16, :].astype(jnp.float32)[:, 0, :]
    one = jnp.sum(jnp.where(seg < 0.5, 1.0, 0.0))
    two = jnp.sum(jnp.where(seg < 1.5, 1.0, 0.0))
    return one.astype(jnp.int32), two.astype(jnp.int32)


def query_geometry(tile, place, starts):
    lane = lax.broadcasted_iota(jnp.int32, (1, QUERIES), 1)
    query_pos = 2 * HALF * (tile * SOURCES + lane // HALF) + HALF * place + lane % HALF
    begin_one, begin_two = starts
    begin = jnp.where(
        query_pos >= begin_two, begin_two, jnp.where(query_pos >= begin_one, begin_one, 0)
    )
    return query_pos, begin


def tile_rows(ref, tile, first_row):
    return jnp.concatenate(
        [
            unpack_pair(ref, tile * SOURCES + pair, first_row, HDIM // 2)
            for pair in range(0, SOURCES, 2)
        ],
        axis=1,
    )


def put_rows(ref, *pieces):
    first = 0
    for piece in pieces:
        ref[first : first + piece.shape[0], :] = piece[...]
        first += piece.shape[0]


def forward_kernel(
    slope_ref,
    place_ref,
    recv_ref,
    tokens_ref,
    far_ref,
    near_ref,
    corner_ref,
    send_ref,
    out_ref,
    lse_ref,
    joined_ref,
    key_ref,
):
    put_rows(joined_ref, tokens_ref, far_ref, near_ref, corner_ref)
    count = recv_ref.shape[0]
    block = 2 * HALF
    slope, place = slope_ref[0], place_ref[0]
    starts = doc_starts(recv_ref)
    for source in range(count):
        key_ref[source * block : (source + 1) * block, :] = (
            recv_ref[source, 0:HDIM, :].astype(jnp.float32).T.astype(jnp.bfloat16)
        )
    values = jnp.concatenate([recv_ref[s, HDIM : 2 * HDIM, :] for s in range(count)], axis=1)
    for tile in range(count // SOURCES):
        reach = (tile + 1) * SOURCES * block
        query = tile_rows(recv_ref, tile, 2 * HDIM).astype(jnp.bfloat16)
        query_pos, begin = query_geometry(tile, place, starts)
        score = masked_scores(key_ref[0:reach, :], query, slope, query_pos, begin, 0, reach)
        high = jnp.max(score, axis=0, keepdims=True)
        weights = jnp.exp(score - high)
        total = jnp.sum(weights, axis=0, keepdims=True)
        out = dot_of(values[:, 0:reach], weights.astype(jnp.bfloat16), 1, 0) / total
        here = slice(tile * QUERIES, (tile + 1) * QUERIES)
        out_ref[:, here] = out
        lse_ref[:, here] = high + jnp.log(total)
        for pair in range(0, SOURCES, 2):
            pack_pair(
                send_ref,
                tile * SOURCES + pair,
                0,
                HDIM // 2,
                out[:, pair * HALF : (pair + 2) * HALF],
            )


def heads_of(ref, first_row):
    return jnp.concatenate(
        [unpack_pair(ref, index, first_row, HDIM // 2) for index in range(0, ref.shape[0], 2)],
        axis=0,
    )


def out_kernel(rank_ref, recv_ref, w_ref, b_ref, part_ref, attn_ref, acc_ref):
    width = w_ref.shape[0]
    turned = heads_of(recv_ref, 0).astype(jnp.bfloat16)
    attn_ref[...] = turned
    acc_ref[...] = dot_of(turned, w_ref[...], 0, 0)
    own = pl.ds(pl.multiple_of(rank_ref[0] * width, width), width)
    acc_ref[:, own] = acc_ref[:, own] + b_ref[...]
    part_ref[...] = acc_ref[...].astype(jnp.bfloat16)


def gelu_pair(value):
    inner = GELU_A * (value + GELU_B * (value * value * value))
    tanh = jnp.tanh(inner)
    half = 0.5 * (1.0 + tanh)
    slope = half + 0.5 * value * (1.0 - tanh * tanh) * (
        GELU_A * (1.0 + 3.0 * GELU_B * (value * value))
    )
    return value * half, slope


def mlp_kernel(
    rank_ref,
    place_ref,
    x_ref,
    cot_ref,
    own_ref,
    other_ref,
    gain_ref,
    bias_ref,
    up_ref,
    b_up_ref,
    down_ref,
    middle_ref,
    act_ref,
    back_ref,
    mine_ref,
    b_grad_ref,
    share_ref,
    swap_ref,
    hidden_ref,
    turn_ref,
    grad_acc,
    mlp_acc,
):
    step = pl.program_id(0)
    rows = act_ref.shape[0]
    width = share_ref.shape[1]

    @pl.when(step == 0)
    def _():
        middle = (
            x_ref[...].astype(jnp.float32)
            + own_ref[...].astype(jnp.float32)
            + other_ref[...].astype(jnp.float32)
        )
        middle_ref[...] = middle
        normed, _ = norm_stats(middle.astype(jnp.bfloat16).astype(jnp.float32))
        hidden_ref[...] = (normed * gain_ref[...] + bias_ref[...]).astype(jnp.bfloat16)
        turn_ref[...] = hidden_ref[...].astype(jnp.float32).T.astype(jnp.bfloat16)
        bit = (place_ref[0] >> UP_BITS[0]) & 1
        put_stripes(mine_ref, 0, turn_ref, UP_BITS[0], UP_BITS[1:], bit)
        first = back_ref.shape[1] - mine_ref.shape[1]
        put_stripes(back_ref, first, turn_ref, UP_BITS[0], UP_BITS[1:], 1 - bit)
        grad_acc[...] = jnp.zeros_like(grad_acc)
        mlp_acc[...] = jnp.zeros_like(mlp_acc)

    pre = jnp.dot(hidden_ref[...], up_ref[...], preferred_element_type=jnp.float32) + b_up_ref[...]
    act, slope = gelu_pair(pre)
    act = act.astype(jnp.bfloat16)
    act_ref[...] = act
    grad_act = dot_of(cot_ref[...], down_ref[...], 1, 1)
    grad_pre = (grad_act * slope).astype(jnp.bfloat16)
    chunk = grad_pre.shape[1]
    back_ref[:, pl.ds(pl.multiple_of(step * chunk, chunk), chunk)] = grad_pre
    b_grad_ref[...] = jnp.sum(grad_pre.astype(jnp.float32), axis=0, keepdims=True)
    grad_acc[...] += dot_of(grad_pre, up_ref[...], 1, 1)
    mlp_acc[...] += jnp.dot(act, down_ref[...], preferred_element_type=jnp.float32)

    @pl.when(step == pl.num_programs(0) - 1)
    def _():
        rank = rank_ref[0]
        swap_ref[:, 0 : 2 * width] = grad_acc[...].astype(jnp.bfloat16)
        swap_ref[:, 2 * width :] = mlp_acc[
            :, pl.ds(pl.multiple_of((1 - rank) * width, width), width)
        ].astype(jnp.bfloat16)
        share_ref[...] = mlp_acc[:, pl.ds(pl.multiple_of(rank * width, width), width)]


def norm_back(whole, normed, inverse, gain):
    scaled = whole * gain
    mean_one = jnp.mean(scaled, axis=-1, keepdims=True)
    mean_two = jnp.mean(scaled * normed, axis=-1, keepdims=True)
    return inverse * (scaled - mean_one - normed * mean_two)


def middle_kernel(
    rank_ref,
    place_ref,
    cot_ref,
    own_ref,
    other_ref,
    middle_ref,
    share_ref,
    gain_ref,
    b_down_ref,
    w_out_ref,
    line_ref,
    line_x_ref,
    mixed_ref,
    grad_ref,
    send_ref,
    mine_ref,
    theirs_ref,
    small_ref,
    joined_ref,
    wide_ref,
    turn_ref,
):
    rows, width = mixed_ref.shape
    put_rows(joined_ref, line_ref, line_x_ref)
    own = pl.ds(pl.multiple_of(rank_ref[0] * width, width), width)
    mixed_ref[...] = (
        middle_ref[:, own]
        + share_ref[...]
        + other_ref[:, 2 * width :].astype(jnp.float32)
        + b_down_ref[...]
    ).astype(jnp.bfloat16)
    whole = own_ref[:, 0 : 2 * width].astype(jnp.float32) + other_ref[:, 0 : 2 * width].astype(
        jnp.float32
    )
    normed, inverse = norm_stats(middle_ref[...].astype(jnp.bfloat16).astype(jnp.float32))
    cot = cot_ref[...].astype(jnp.float32)
    grad = cot + norm_back(whole, normed, inverse, gain_ref[...])
    low = grad.astype(jnp.bfloat16)
    turn_ref[...] = grad.T.astype(jnp.bfloat16)
    bit = (place_ref[0] >> UP_BITS[0]) & 1
    put_stripes(mine_ref, 0, turn_ref, UP_BITS[0], UP_BITS[1:], bit)
    put_stripes(theirs_ref, 0, turn_ref, UP_BITS[0], UP_BITS[1:], 1 - bit)
    wide_ref[0:1] = jnp.sum(whole * normed, axis=0, keepdims=True)
    wide_ref[1:2] = jnp.sum(whole, axis=0, keepdims=True)
    wide_ref[2:3] = jnp.sum(grad, axis=0, keepdims=True)
    wide_ref[3:4] = jnp.sum(cot, axis=0, keepdims=True)
    wide_ref[8:, :] = grad
    small_ref[...] = wide_ref[0:8, own]
    grad_ref[...] = wide_ref[8:, own]
    back = dot_of(w_out_ref[...], low, 1, 1).astype(jnp.bfloat16).astype(jnp.float32)
    for head in range(width // HDIM):
        pack_pair(send_ref, 2 * head, 0, HDIM // 2, back[head * HDIM : (head + 1) * HDIM])


def backward_kernel(
    slope_ref,
    place_ref,
    recv_ref,
    grad_ref,
    out_ref,
    lse_ref,
    send_ref,
    low_ref,
    key_ref,
    value_ref,
    key_acc,
    value_acc,
):
    count = recv_ref.shape[0]
    block = 2 * HALF
    slope, place = slope_ref[0], place_ref[0]
    starts = doc_starts(recv_ref)
    for source in range(count):
        there = slice(source * block, (source + 1) * block)
        key_ref[there, :] = recv_ref[source, 0:HDIM, :].astype(jnp.float32).T.astype(jnp.bfloat16)
        value_ref[there, :] = (
            recv_ref[source, HDIM : 2 * HDIM, :].astype(jnp.float32).T.astype(jnp.bfloat16)
        )
    keys_turned = jnp.concatenate([recv_ref[s, 0:HDIM, :] for s in range(count)], axis=1)
    key_acc[...] = jnp.zeros_like(key_acc)
    value_acc[...] = jnp.zeros_like(value_acc)
    for tile in range(count // SOURCES):
        reach = (tile + 1) * SOURCES * block
        here = slice(tile * QUERIES, (tile + 1) * QUERIES)
        query = tile_rows(recv_ref, tile, 2 * HDIM).astype(jnp.bfloat16)
        grad_wide = tile_rows(grad_ref, tile, 0)
        grad = grad_wide.astype(jnp.bfloat16)
        delta = jnp.sum(grad_wide * out_ref[:, here], axis=0, keepdims=True)
        query_pos, begin = query_geometry(tile, place, starts)
        score = masked_scores(key_ref[0:reach, :], query, slope, query_pos, begin, 0, reach)
        prob = jnp.exp(score - lse_ref[:, here])
        grad_prob = dot_of(value_ref[0:reach, :], grad, 1, 0)
        grad_score = (prob * (grad_prob - delta)).astype(jnp.bfloat16)
        key_acc[:, 0:reach] += dot_of(query, grad_score, 1, 1)
        value_acc[:, 0:reach] += dot_of(grad, prob.astype(jnp.bfloat16), 1, 1)
        query_grad = dot_of(keys_turned[:, 0:reach], grad_score, 1, 0) * (1.0 / math.sqrt(HDIM))
        query_grad = query_grad.astype(jnp.bfloat16).astype(jnp.float32)
        for pair in range(0, SOURCES, 2):
            index = tile * SOURCES + pair
            piece = query_grad[:, pair * HALF : (pair + 2) * HALF]
            pack_pair(send_ref, index, 2 * HDIM, HDIM // 2, piece)
            other = pltpu.roll(piece, HALF, 1)
            lane = lax.broadcasted_iota(jnp.int32, piece.shape, 1)
            mine = lane // HALF == place
            is_low = place == 0
            low_ref[0:HDIM, index * block : (index + 1) * block] = jnp.where(
                mine, jnp.where(is_low, piece, other), 0.0
            ).astype(jnp.bfloat16)
            low_ref[0:HDIM, (index + 1) * block : (index + 2) * block] = jnp.where(
                mine, jnp.where(is_low, other, piece), 0.0
            ).astype(jnp.bfloat16)
    low_ref[HDIM : 2 * HDIM, :] = key_acc[...].astype(jnp.bfloat16)
    low_ref[2 * HDIM :, :] = value_acc[...].astype(jnp.bfloat16)
    for source in range(count):
        there = slice(source * block, (source + 1) * block)
        send_ref[source, 0 : 2 * HDIM, :] = low_ref[HDIM:, there]


def weight_kernel(
    rank_ref, device_ref, gain_ref, bias_ref, grad_ref, *refs
):
    own_refs, other_refs = refs[:2], refs[2:4]
    send_ref, wide_ref, order_ref, acc_ref = refs[4:]
    block = 2 * HALF
    first = 0
    for own_ref, other_ref in zip(own_refs, other_refs):
        put_halves(wide_ref.at[first : first + own_ref.shape[0]], rank_ref[0], own_ref, other_ref)
        first += own_ref.shape[0]
    for position, code in enumerate(GATHERED):
        source = device_ref[0] ^ code
        order_ref[:, position * block : (position + 1) * block] = grad_ref[
            :, pl.ds(pl.multiple_of(source * block, block), block)
        ]
    acc_ref[...] = jnp.zeros_like(acc_ref)

    def add(step, carry):
        here = pl.ds(pl.multiple_of(step * 2 * block, 2 * block), 2 * block)
        normed, _ = norm_stats(wide_ref[here, :].astype(jnp.float32))
        hidden = (normed * gain_ref[...] + bias_ref[...]).astype(jnp.bfloat16)
        acc_ref[...] += jnp.dot(order_ref[:, here], hidden, preferred_element_type=jnp.float32)
        return carry

    lax.fori_loop(0, first // (2 * block), add, 0)
    for index in range(0, send_ref.shape[0], 2):
        pack_pair(
            send_ref, index, 0, 3 * HDIM // 2, acc_ref[:, index * HALF : (index + 2) * HALF]
        )


def hidden_kernel(recv_ref, w_ref, part_ref, b_ref, acc_ref):
    step = pl.program_id(0)
    count = recv_ref.shape[0]

    @pl.when(step == 0)
    def _():
        acc_ref[...] = jnp.zeros_like(acc_ref)

    def add(turned):
        acc_ref[...] += dot_of(turned, w_ref[0], 0, 1)
        ones = jnp.ones((8, turned.shape[1]), jnp.bfloat16)
        b_ref[0] = dot_of(ones, turned, 1, 1)

    @pl.when(step == 0)
    def _():
        add(heads_of(recv_ref, 2 * HDIM).astype(jnp.bfloat16))

    for which in (1, 2):

        @pl.when(step == which)
        def _(which=which):
            span = slice((which - 1) * HDIM, which * HDIM)
            add(
                jnp.concatenate(
                    [
                        recv_ref[index, span, :].astype(jnp.float32)
                        + recv_ref[index + 1, span, :].astype(jnp.float32)
                        for index in range(0, count, 2)
                    ],
                    axis=0,
                ).astype(jnp.bfloat16)
            )

    @pl.when(step == 2)
    def _():
        part_ref[...] = acc_ref[...].astype(jnp.bfloat16)


def input_kernel(rank_ref, x_ref, own_ref, other_ref, gain_ref, grad_ref, out_ref, small_ref, wide_ref):
    rows, width = out_ref.shape
    own = pl.ds(pl.multiple_of(rank_ref[0] * width, width), width)
    normed, inverse = norm_stats(x_ref[...].astype(jnp.float32))
    whole = own_ref[...].astype(jnp.float32) + other_ref[...].astype(jnp.float32)
    wide_ref[0:1] = jnp.sum(whole * normed, axis=0, keepdims=True)
    wide_ref[1:2] = jnp.sum(whole, axis=0, keepdims=True)
    wide_ref[8:, :] = norm_back(whole, normed, inverse, gain_ref[...])
    small_ref[...] = wide_ref[0:8, own]
    out_ref[...] = (grad_ref[...] + wide_ref[8:, own]).astype(jnp.bfloat16)


def call(
    kernel,
    outs,
    ins,
    scratch=(),
    grid=None,
    in_specs=None,
    out_specs=None,
    after=(),
    mebibytes=16,
    flops=10**8,
):
    vmem = pl.BlockSpec(memory_space=pltpu.VMEM)
    smem = pl.BlockSpec(memory_space=pltpu.SMEM)
    specs = list(in_specs or [smem if value.ndim == 1 else vmem for value in ins])
    options = {} if grid is None else {"grid": grid}
    taken = len(ins)
    waits = len(after)

    def body(*refs):
        kernel(*refs[:taken], *refs[taken + waits :])

    return pl.pallas_call(
        body,
        out_shape=[jax.ShapeDtypeStruct(shape, dtype) for shape, dtype in outs],
        in_specs=specs + [pl.BlockSpec(memory_space=pl.ANY)] * waits,
        out_specs=out_specs or [vmem] * len(outs),
        scratch_shapes=list(scratch),
        compiler_params=pltpu.CompilerParams(vmem_limit_bytes=mebibytes * 1024 * 1024),
        cost_estimate=pl.CostEstimate(
            flops=flops // 10**4, bytes_accessed=1024, transcendentals=0
        ),
        **options,
    )(*ins, *after)


def stripe_rows(ref, first, count):
    side = 2 * HALF
    blocks = [
        ref[:, pl.ds(pl.multiple_of(first + part * side, side), side)]
        for part in range(count // side)
    ]
    return jnp.concatenate(blocks, axis=0)


def wide_product(bit, piece, left_ref, left_got_ref, right_ref, right_got_ref):
    turned, columns, got_first = piece
    half = left_ref.shape[1] // 2
    if turned:
        right = jnp.concatenate([right_ref[...], right_got_ref[...]], axis=1)
    else:
        right = jnp.concatenate([right_ref[:, 0:columns], right_got_ref[:, 0:columns]], axis=0)
    left = jnp.concatenate(
        [
            stripe_rows(left_ref, bit * half, half),
            stripe_rows(left_got_ref, got_first + bit * half, half),
        ],
        axis=1,
    )
    return dot_of(left, right, 1, 1 if turned else 0)


def group_products(groups, place_ref, ins, wanted):
    at = 0
    for number, (order, pieces) in enumerate(groups):
        bit = bit_at(place_ref, order[1])
        first = 0
        for piece in pieces:
            here = slice(first, first + piece[1])
            first = here.stop
            yield number, here, wide_product(
                bit if wanted else 1 - bit, piece, *ins[4 * at : 4 * at + 4]
            )
            at += 1


def split_rows(bit, acc_ref, send_ref, keep_ref):
    half = keep_ref.shape[0]
    send_ref[...] = acc_ref[pl.ds(pl.multiple_of((1 - bit) * half, half), half), :].astype(
        send_ref.dtype
    )
    keep_ref[...] = acc_ref[pl.ds(pl.multiple_of(bit * half, half), half), :].astype(
        keep_ref.dtype
    )


def bit_at(place_ref, bit):
    return (place_ref[0] >> bit) & 1


def product_kernel(groups, place_ref, *refs):
    kinds = len(groups)
    for number, here, value in group_products(groups, place_ref, refs[:-kinds], False):
        refs[number - kinds][:, here] = value.astype(jnp.bfloat16)


def product_add_kernel(groups, place_ref, *refs):
    kinds = len(groups)
    got, sends, keeps, accs = (
        refs[first * kinds : (first + 1) * kinds or None] for first in range(-4, 0)
    )
    for number, here, value in group_products(groups, place_ref, refs[: -4 * kinds], True):
        accs[number][:, here] = value + got[number][:, here].astype(jnp.float32)
    for number, (order, _) in enumerate(groups):
        split_rows(bit_at(place_ref, order[2]), accs[number], sends[number], keeps[number])


def add_kernel(groups, place_ref, *refs):
    kinds = len(groups)
    send_ref, keep_ref, acc_ref = refs[2 * kinds :]
    first = 0
    for number in range(kinds):
        here = slice(first, first + refs[number].shape[1])
        first = here.stop
        acc_ref[:, here] = refs[number][...].astype(jnp.float32) + refs[kinds + number][
            ...
        ].astype(jnp.float32)
    split_rows(bit_at(place_ref, groups[0][0][3]), acc_ref, send_ref, keep_ref)


def last_kernel(keep_ref, got_ref, *out_refs):
    first = 0
    for ref in out_refs:
        here = slice(first, first + ref.shape[1])
        first = here.stop
        ref[...] = keep_ref[:, here].astype(jnp.float32) + got_ref[:, here].astype(jnp.float32)


def held(value, after):
    return pl.pallas_call(
        lambda *refs: None,
        out_shape=jax.ShapeDtypeStruct(value.shape, value.dtype),
        in_specs=[pl.BlockSpec(memory_space=pl.ANY)] * (1 + len(after)),
        out_specs=pl.BlockSpec(memory_space=pl.ANY),
        input_output_aliases={0: 0},
    )(value, *after)


def swap_over(value, bit, count):
    return lax.ppermute(value, "ctx", [(place, place ^ (1 << bit)) for place in range(count)])


class Reductions:
    def __init__(self, groups, device, count, ins):
        self.groups, self.device, self.count, self.ins = groups, device, count, ins
        self.columns = [sum(piece[1] for piece in pieces) for _, pieces in groups]
        self.rows = ins[0].shape[1] // 2

    def shapes(self, rows, dtype):
        return [((rows, columns), dtype) for columns in self.columns]

    def swap(self, sent, stage):
        return [
            swap_over(value, order[stage], self.count)
            for value, (order, _) in zip(sent, self.groups)
        ]

    def first(self, after):
        sent = call(
            functools.partial(product_kernel, self.groups),
            self.shapes(self.rows, jnp.bfloat16),
            [self.device] + self.ins,
            after=after,
            mebibytes=60,
            flops=10**15,
        )
        self.got = self.swap(sent, 1)
        return sent

    def second(self, after):
        half = self.rows // 2
        kinds = len(self.groups)
        results = call(
            functools.partial(product_add_kernel, self.groups),
            self.shapes(half, jnp.bfloat16) * 2,
            [self.device] + self.ins + self.got,
            scratch=[pltpu.VMEM((self.rows, columns), jnp.float32) for columns in self.columns],
            after=after,
            mebibytes=60,
            flops=10**15,
        )
        self.keep = results[kinds:]
        self.got = self.swap(results[:kinds], 2)
        return results[:kinds]

    def third(self, after):
        quarter = self.rows // 4
        wide = sum(self.columns)
        sent, self.keep = call(
            functools.partial(add_kernel, self.groups),
            [((quarter, wide), jnp.bfloat16)] * 2,
            [self.device] + list(self.keep) + list(self.got),
            scratch=[pltpu.VMEM((2 * quarter, wide), jnp.float32)],
            after=after,
            mebibytes=60,
            flops=2 * 10**9,
        )
        self.got = swap_over(sent, self.groups[0][0][3], self.count)
        return [sent]

    def last(self):
        return call(
            last_kernel,
            [
                ((self.rows // 4, piece[1]), jnp.float32)
                for _, pieces in self.groups
                for piece in pieces
            ],
            [self.keep, self.got],
            mebibytes=60,
            flops=10**9,
        )


def on_device_paired(
    tokens,
    segment_ids,
    ln1_gain,
    ln1_bias,
    w_qkv,
    b_qv,
    w_out,
    b_out,
    ln2_gain,
    ln2_bias,
    w_up,
    b_up,
    w_down,
    b_down,
    cotangent,
    count,
):
    bf16, f32 = jnp.bfloat16, jnp.float32
    rows, width = tokens.shape
    model = w_out.shape[1]
    hidden = w_up.shape[1]
    heads = width // HDIM
    block = 2 * HALF
    all_tokens = count * rows
    tp_rank = lax.axis_index("tp")
    place = lax.axis_index("ctx")
    rank = tp_rank.reshape(1)
    side = (place % 2).reshape(1)
    slope = head_slopes(tp_rank * heads + place // 2, 1)
    gain_one, bias_one = ln1_gain.reshape(1, model), ln1_bias.reshape(1, model)
    gain_two, bias_two = ln2_gain.reshape(1, model), ln2_bias.reshape(1, model)
    other_core = lambda value: lax.ppermute(value, "tp", [(0, 1), (1, 0)])
    to_heads = lambda value: lax.all_to_all(value, "ctx", 0, 0, tiled=True)
    smem = pl.BlockSpec(memory_space=pltpu.SMEM)
    whole = lambda *shape: pl.BlockSpec(shape, lambda step: (0,) * len(shape))

    device = place.reshape(1)
    sent, full_in, full_cot, cot_mine, cot_theirs = call(
        qkv_kernel,
        [
            ((count, FWD_ROWS, rows), bf16),
            ((rows, model), bf16),
            ((rows, model), bf16),
            ((rows, model // 2), bf16),
            ((rows, model // 2), bf16),
        ],
        [
            rank,
            device,
            tokens,
            other_core(tokens),
            cotangent,
            other_core(cotangent),
            gain_one,
            bias_one,
            w_qkv,
            b_qv,
            segment_ids.reshape(1, rows),
        ],
        scratch=[pltpu.VMEM((rows, model), bf16), pltpu.VMEM((model, rows), bf16)],
        grid=(3,),
        in_specs=[smem, smem]
        + [whole(rows, width)] * 4
        + [
            whole(1, model),
            whole(1, model),
            pl.BlockSpec((1, model, width), lambda step: (step, 0, 0)),
            whole(2, width),
            whole(1, rows),
        ],
        out_specs=[
            whole(count, FWD_ROWS, rows),
            whole(rows, model),
            whole(rows, model),
            whole(rows, model // 2),
            whole(rows, model // 2),
        ],
        mebibytes=60,
        flops=3 * 10**9,
    )
    cot_got = swap_over(cot_theirs, DOWN_BITS[0], count)
    bit_x, bit_y, bit_z, bit_far = range(4)
    far, near = swap_over(tokens, bit_far, count), swap_over(tokens, bit_z, count)
    corner = swap_over(far, bit_z, count)
    got = to_heads(held(sent, [far, near]))
    attn_sent, attn_raw, lse, line = call(
        forward_kernel,
        [
            ((count, HDIM // 2, rows), bf16),
            ((HDIM, all_tokens // 2), f32),
            ((1, all_tokens // 2), f32),
            ((4 * rows, width), bf16),
        ],
        [slope, side, got, tokens, far, near, corner],
        scratch=[pltpu.VMEM((all_tokens, HDIM), bf16)],
        mebibytes=24,
        flops=4 * 10**9,
    )
    line_x = swap_over(line, bit_x, count)
    attn_got = to_heads(attn_sent)
    part, attn_turned = call(
        out_kernel,
        [((rows, model), bf16), ((width, rows), bf16)],
        [rank, attn_got, w_out, b_out.reshape(1, width)],
        scratch=[pltpu.VMEM((rows, model), f32)],
    )
    chunk = 512
    middle, act, grad_pre, h_mine, grad_b_up, share, swap = call(
        mlp_kernel,
        [
            ((rows, model), f32),
            ((rows, hidden), bf16),
            ((rows, hidden + model // 2), bf16),
            ((rows, model // 2), bf16),
            ((1, hidden), f32),
            ((rows, width), f32),
            ((rows, model + width), bf16),
        ],
        [
            rank,
            device,
            full_in,
            full_cot,
            part,
            other_core(part),
            gain_two,
            bias_two,
            w_up,
            b_up.reshape(1, hidden),
            w_down,
        ],
        grid=(hidden // chunk,),
        in_specs=[smem, smem]
        + [whole(rows, model)] * 4
        + [
            whole(1, model),
            whole(1, model),
            pl.BlockSpec((model, chunk), lambda step: (0, step)),
            pl.BlockSpec((1, chunk), lambda step: (0, step)),
            pl.BlockSpec((chunk, model), lambda step: (step, 0)),
        ],
        out_specs=[
            whole(rows, model),
            pl.BlockSpec((rows, chunk), lambda step: (0, step)),
            whole(rows, hidden + model // 2),
            whole(rows, model // 2),
            pl.BlockSpec((1, chunk), lambda step: (0, step)),
            whole(rows, width),
            whole(rows, model + width),
        ],
        scratch=[
            pltpu.VMEM((rows, model), bf16),
            pltpu.VMEM((model, rows), bf16),
            pltpu.VMEM((rows, model), f32),
            pltpu.VMEM((rows, model), f32),
        ],
        mebibytes=56,
        flops=7 * 10**9,
    )
    mixed, grad_mid, grad_sent, low_mine, out_theirs, small_two, plane = call(
        middle_kernel,
        [
            ((rows, width), bf16),
            ((rows, width), f32),
            ((count, HDIM // 2, rows), bf16),
            ((rows, model // 2), bf16),
            ((rows, model // 2), bf16),
            ((8, width), f32),
            ((8 * rows, width), bf16),
        ],
        [
            rank,
            device,
            full_cot,
            swap,
            other_core(swap),
            middle,
            share,
            gain_two,
            b_down.reshape(1, width),
            w_out,
            line,
            line_x,
        ],
        scratch=[pltpu.VMEM((rows + 8, model), f32), pltpu.VMEM((model, rows), bf16)],
        mebibytes=60,
        flops=2 * 10**9,
    )
    back_other = swap_over(grad_pre, UP_BITS[0], count)
    reductions = Reductions(
        (
            (DOWN_BITS, ((False, hidden, 0),)),
            (UP_BITS, ((False, hidden, hidden), (True, width, 0))),
        ),
        device,
        count,
        [cot_mine, cot_got, act, swap_over(act, DOWN_BITS[0], count)]
        + [h_mine, back_other, grad_pre, back_other]
        + [low_mine, swap_over(out_theirs, UP_BITS[0], count)]
        + [attn_turned, swap_over(attn_turned, UP_BITS[0], count)],
    )
    grad_got = to_heads(grad_sent)
    gathered = [plane, swap_over(plane, bit_y, count)]
    gathered += [other_core(value) for value in gathered]
    first_sent = reductions.first([])
    back_sent, back_low = call(
        backward_kernel,
        [((count, SEG_ROW, rows), bf16), ((3 * HDIM, all_tokens), bf16)],
        [slope, side, got, grad_got, attn_raw, lse],
        scratch=[
            pltpu.VMEM((all_tokens, HDIM), bf16),
            pltpu.VMEM((all_tokens, HDIM), bf16),
            pltpu.VMEM((HDIM, all_tokens), f32),
            pltpu.VMEM((HDIM, all_tokens), f32),
        ],
        after=[first_sent[0]],
        mebibytes=56,
        flops=10**10,
    )
    (weight_sent,) = call(
        weight_kernel,
        [((count, 3 * HDIM // 2, rows), bf16)],
        [rank, device, gain_one, bias_one, back_low] + gathered,
        scratch=[
            pltpu.VMEM((all_tokens, model), bf16),
            pltpu.VMEM((3 * HDIM, all_tokens), bf16),
            pltpu.VMEM((3 * HDIM, model), f32),
        ],
        mebibytes=56,
        flops=6 * 10**9,
    )
    weight_got = to_heads(weight_sent)
    second_sent = reductions.second([weight_sent])
    third_sent = reductions.third([weight_got])
    back_got = to_heads(back_sent)
    part_one, sums = call(
        hidden_kernel,
        [
            ((rows, model), bf16),
            ((3, 8, width), f32),
        ],
        [back_got, w_qkv],
        grid=(3,),
        in_specs=[
            whole(count, SEG_ROW, rows),
            pl.BlockSpec((1, model, width), lambda step: (step, 0, 0)),
        ],
        out_specs=[
            whole(rows, model),
            pl.BlockSpec((1, 8, width), lambda step: (step, 0, 0)),
        ],
        scratch=[pltpu.VMEM((rows, model), f32)],
        after=[second_sent[0]],
        flops=3 * 10**9,
    )
    input_grad, small_one = call(
        input_kernel,
        [((rows, width), bf16), ((8, width), f32)],
        [rank, full_in, part_one, other_core(part_one), gain_one, grad_mid],
        scratch=[pltpu.VMEM((rows + 8, model), f32)],
        after=[third_sent[0]],
    )
    grad_down, grad_up, grad_out = reductions.last()
    stripe = model // count
    grad_qkv = (
        weight_got.astype(f32)
        .reshape(heads, 2, 3 * HDIM // 2, 2 * stripe)
        .sum(axis=1)
        .reshape(heads, 3 * HDIM // 2, 2, stripe)
        .transpose(0, 2, 1, 3)
        .reshape(heads, 3, HDIM, stripe)
        .transpose(1, 3, 0, 2)
        .reshape(3, stripe, width)
    )
    share_w = width // count
    vectors = jnp.concatenate(
        [
            small_one[0:2].reshape(2, count, share_w),
            sums[0:3:2, 0].reshape(2, count, share_w),
            small_two[0:4].reshape(4, count, share_w),
            grad_b_up.reshape(count, -1, share_w).transpose(1, 0, 2),
        ],
        axis=0,
    )
    lanes = vectors.shape[0] * share_w
    spread = vectors.transpose(1, 0, 2).reshape(count, 1, lanes)
    total = jnp.sum(to_heads(spread), axis=0).reshape(-1, share_w)
    return (
        mixed,
        input_grad,
        total[0],
        total[1],
        grad_qkv,
        total[2:4],
        grad_out.T,
        total[6],
        total[4],
        total[5],
        grad_up,
        total[8:].reshape(-1),
        grad_down.T,
        total[7],
    )


def paired(mesh, arrays):
    sizes = dict(mesh.shape)
    count, cores = sizes["ctx"], sizes["tp"]
    rows = arrays[0].shape[0] // count
    return (
        cores == 2
        and count == 16
        and rows == 2 * HALF
        and count * cores == 2 * HEADS
        and arrays[0].shape[1] == HEADS * HDIM
    )


def solution(mesh):
    in_specs = (
        P("ctx", "tp"),
        P("ctx"),
        P(),
        P(),
        P(None, None, "tp"),
        P(None, "tp"),
        P("tp", None),
        P("tp"),
        P(),
        P(),
        P(None, "tp"),
        P("tp"),
        P("tp", None),
        P("tp"),
        P("ctx", "tp"),
    )
    out_specs = (
        P("ctx", "tp"),
        P("ctx", "tp"),
        P(("tp", "ctx")),
        P(("tp", "ctx")),
        P(None, "ctx", "tp"),
        P(None, ("tp", "ctx")),
        P("tp", "ctx"),
        P(("tp", "ctx")),
        P(("tp", "ctx")),
        P(("tp", "ctx")),
        P("ctx", "tp"),
        P(("tp", "ctx")),
        P("tp", "ctx"),
        P(("tp", "ctx")),
    )

    def run(*arrays):
        if paired(mesh, arrays):
            body = functools.partial(on_device_paired, count=dict(mesh.shape)["ctx"])
        else:
            body = on_device
        return jax.shard_map(
            body, mesh=mesh, in_specs=in_specs, out_specs=out_specs, check_vma=False
        )(*arrays)

    return run
```

```python
import functools
import math

import jax
import jax.numpy as jnp
from jax import lax
from jax.experimental import pallas as pl
from jax.experimental.pallas import tpu as pltpu
from jax.sharding import PartitionSpec as P

HEADS = 16
HDIM = 64


norm_eps = 1e-05
mask_fill = -1e30
score_block = 512

HALF = 64
SOURCES = 4
QUERIES = SOURCES * HALF
SEG_ROW = 5 * HDIM // 2
FWD_ROWS = SEG_ROW + 16
GELU_A = math.sqrt(2.0 / math.pi)
GELU_B = 0.044715

DOWN_BITS = (0, 1, 2, 3)
UP_BITS = (2, 0, 1, 3)
GATHERED = (0, 8, 4, 12, 1, 9, 5, 13, 2, 10, 6, 14, 3, 11, 7, 15)


def head_slopes(first_head, head_count):
    index_list = first_head + jnp.arange(head_count, dtype=jnp.int32)
    return jnp.exp2(-8.0 * (index_list + 1).astype(jnp.float32) / HEADS)


def pair_scores(query_heads, query_pos, query_seg, key_heads, key_pos, key_seg, slopes):
    logits = jnp.einsum(
        "qhd,khd->hqk", query_heads, key_heads, preferred_element_type=jnp.float32
    ) / math.sqrt(HDIM)
    distance = (key_pos[None, :] - query_pos[:, None]).astype(jnp.float32)
    allowed = (key_pos[None, :] <= query_pos[:, None]) & (key_seg[None, :] == query_seg[:, None])
    return (
        jnp.where(allowed[None], logits + slopes[:, None, None] * distance[None], mask_fill),
        allowed,
    )


def block_grads(
    query_heads,
    query_pos,
    query_seg,
    grad_heads,
    lse_rows,
    delta_rows,
    key_heads,
    value_heads,
    key_pos,
    key_seg,
    slopes,
):
    score, allowed = pair_scores(
        query_heads, query_pos, query_seg, key_heads, key_pos, key_seg, slopes
    )
    prob = jnp.where(allowed[None], jnp.exp(score - lse_rows.T[:, :, None]), 0.0)
    grad_prob = jnp.einsum(
        "qhd,khd->hqk", grad_heads, value_heads, preferred_element_type=jnp.float32
    )
    grad_score = (prob * (grad_prob - delta_rows.T[:, :, None])).astype(jnp.bfloat16)
    return (prob.astype(jnp.bfloat16), grad_score)


def over_blocks(row_count, step_fn, state_now):
    return lax.fori_loop(
        0,
        row_count // score_block,
        lambda number, inner_state: step_fn(number * score_block, score_block, inner_state),
        state_now,
    )


def seg_at(seg_array, where_row):
    return lax.dynamic_slice_in_dim(seg_array, where_row, 1)[0]


def gather_features(local_rows):
    return lax.all_gather(local_rows, "tp", axis=1, tiled=True)


def norm_stats(full_rows):
    center = full_rows - jnp.mean(full_rows, axis=-1, keepdims=True)
    inverse = lax.rsqrt(jnp.mean(center * center, axis=-1, keepdims=True) + norm_eps)
    return (center * inverse, inverse)


def norm_backward(part_grad, normed, inverse, gain, tp_rank, local_width):
    offset = tp_rank * local_width
    whole_grad = lax.psum(part_grad.astype(jnp.bfloat16), "tp").astype(jnp.float32)
    scaled = whole_grad * gain
    mean_one = jnp.mean(scaled, axis=-1, keepdims=True)
    mean_two = jnp.mean(scaled * normed, axis=-1, keepdims=True)
    input_grad = lax.dynamic_slice_in_dim(
        inverse * (scaled - mean_one - normed * mean_two), offset, local_width, 1
    )
    share_grad = lax.dynamic_slice_in_dim(whole_grad, offset, local_width, 1)
    normed_share = lax.dynamic_slice_in_dim(normed, offset, local_width, 1)
    gain_grad = jnp.sum(share_grad * normed_share, axis=0)
    bias_grad = jnp.sum(share_grad, axis=0)
    return (input_grad, gain_grad, bias_grad)


def on_device(
    tokens,
    segment_ids,
    ln1_gain,
    ln1_bias,
    w_qkv,
    b_qv,
    w_out,
    b_out,
    ln2_gain,
    ln2_bias,
    w_up,
    b_up,
    w_down,
    b_down,
    cotangent,
):
    local_rows, local_width = tokens.shape
    heads_local = local_width // HDIM
    tp_rank = lax.axis_index("tp")
    ctx_rank = lax.axis_index("ctx")
    slopes = head_slopes(tp_rank * heads_local, heads_local)
    own_pos = ctx_rank * local_rows + jnp.arange(local_rows, dtype=jnp.int32)
    own_first_seg = segment_ids[0]
    own_last_seg = segment_ids[-1]
    full_in = gather_features(tokens)
    normed_one, inverse_one = norm_stats(full_in.astype(jnp.float32))
    hidden_one = (normed_one * ln1_gain + ln1_bias).astype(jnp.bfloat16)
    projected = jnp.einsum("td,cde->cte", hidden_one, w_qkv, preferred_element_type=jnp.float32)
    query_rows = (projected[0] + b_qv[0]).astype(jnp.bfloat16)
    key_rows = projected[1].astype(jnp.bfloat16)
    value_rows = (projected[2] + b_qv[1]).astype(jnp.bfloat16)
    query_heads = query_rows.reshape(local_rows, heads_local, HDIM)
    key_heads = key_rows.reshape(local_rows, heads_local, HDIM)
    value_heads = value_rows.reshape(local_rows, heads_local, HDIM)
    start_state = (
        jnp.full((heads_local, local_rows), mask_fill, jnp.float32),
        jnp.zeros((heads_local, local_rows), jnp.float32),
        jnp.zeros((heads_local, local_rows, HDIM), jnp.float32),
    )
    piece_keys = lax.all_gather(key_rows, "ctx", axis=0, tiled=True)
    piece_values = lax.all_gather(value_rows, "ctx", axis=0, tiled=True)
    piece_seg = lax.all_gather(segment_ids, "ctx", axis=0, tiled=True)

    def forward_one_block(offset, size_each, inner_state):

        def attend(running):
            high_now, total_now, acc_now = running
            block_keys = lax.dynamic_slice_in_dim(piece_keys, offset, size_each).reshape(
                size_each, heads_local, HDIM
            )
            block_values = lax.dynamic_slice_in_dim(piece_values, offset, size_each).reshape(
                size_each, heads_local, HDIM
            )
            block_seg = lax.dynamic_slice_in_dim(piece_seg, offset, size_each)
            key_pos = offset + jnp.arange(size_each, dtype=jnp.int32)
            score, allowed = pair_scores(
                query_heads, own_pos, segment_ids, block_keys, key_pos, block_seg, slopes
            )
            high_new = jnp.maximum(high_now, jnp.max(score, axis=-1))
            weights = jnp.where(allowed[None], jnp.exp(score - high_new[:, :, None]), 0.0)
            factor = jnp.exp(high_now - high_new)
            total_new = total_now * factor + jnp.sum(weights, axis=-1)
            acc_new = acc_now * factor[:, :, None] + jnp.einsum(
                "hqk,khd->hqd",
                weights.astype(jnp.bfloat16),
                block_values,
                preferred_element_type=jnp.float32,
            )
            return (high_new, total_new, acc_new)

        needed = (offset <= own_pos[-1]) & (
            seg_at(piece_seg, offset + size_each - 1) >= own_first_seg
        )
        return lax.cond(needed, attend, lambda running: running, inner_state)

    high_fin, total_fin, acc_fin = over_blocks(piece_keys.shape[0], forward_one_block, start_state)
    attn_raw = jnp.transpose(acc_fin / total_fin[:, :, None], (1, 0, 2)).reshape(
        local_rows, local_width
    )
    lse_rows = (high_fin + jnp.log(total_fin)).T
    attn_low = attn_raw.astype(jnp.bfloat16)
    attn_share = lax.psum_scatter(
        jnp.dot(attn_low, w_out, preferred_element_type=jnp.float32).astype(jnp.bfloat16),
        "tp",
        scatter_dimension=1,
        tiled=True,
    ).astype(jnp.float32)
    middle = tokens.astype(jnp.float32) + attn_share + b_out
    full_mid = gather_features(middle.astype(jnp.bfloat16))
    normed_two, inverse_two = norm_stats(full_mid.astype(jnp.float32))
    hidden_two = (normed_two * ln2_gain + ln2_bias).astype(jnp.bfloat16)
    pre_act = jnp.dot(hidden_two, w_up, preferred_element_type=jnp.float32) + b_up
    gelu_out, gelu_back = jax.vjp(
        lambda pre_value: jax.nn.gelu(pre_value, approximate=True), pre_act
    )
    activated = gelu_out.astype(jnp.bfloat16)
    mlp_share = lax.psum_scatter(
        jnp.dot(activated, w_down, preferred_element_type=jnp.float32).astype(jnp.bfloat16),
        "tp",
        scatter_dimension=1,
        tiled=True,
    ).astype(jnp.float32)
    output = middle + mlp_share + b_down
    contract_rows = (((0,), (0,)), ((), ()))
    contract_cols = (((1,), (1,)), ((), ()))
    out_grad = cotangent.astype(jnp.float32)
    full_cot = gather_features(cotangent)
    grad_down = lax.dot_general(
        activated, full_cot, contract_rows, preferred_element_type=jnp.float32
    )
    grad_act = lax.dot_general(full_cot, w_down, contract_cols, preferred_element_type=jnp.float32)
    grad_pre = gelu_back(grad_act)[0].astype(jnp.bfloat16)
    grad_bup = jnp.sum(grad_pre.astype(jnp.float32), axis=0)
    grad_up = lax.dot_general(
        hidden_two, grad_pre, contract_rows, preferred_element_type=jnp.float32
    )
    part_two = lax.dot_general(grad_pre, w_up, contract_cols, preferred_element_type=jnp.float32)
    grad_mid_norm, grad_gain_two, grad_bias_two = norm_backward(
        part_two, normed_two, inverse_two, ln2_gain, tp_rank, local_width
    )
    grad_middle = out_grad + grad_mid_norm
    grad_bdown = jnp.sum(out_grad, axis=0)
    grad_bout = jnp.sum(grad_middle, axis=0)
    full_back = gather_features(grad_middle.astype(jnp.bfloat16))
    grad_wout = lax.dot_general(
        attn_low, full_back, contract_rows, preferred_element_type=jnp.float32
    )
    grad_attn = lax.dot_general(
        full_back, w_out, contract_cols, preferred_element_type=jnp.float32
    ).astype(jnp.bfloat16)
    grad_heads = grad_attn.reshape(local_rows, heads_local, HDIM)
    delta_rows = jnp.sum(
        grad_heads.astype(jnp.float32) * attn_raw.reshape(local_rows, heads_local, HDIM), axis=-1
    )
    query_zero = jnp.zeros((local_rows, heads_local, HDIM), jnp.float32)
    back_state = (query_zero,)
    backward_piece_keys = lax.all_gather(key_rows, "ctx", axis=0, tiled=True)
    backward_piece_values = lax.all_gather(value_rows, "ctx", axis=0, tiled=True)
    backward_piece_seg = lax.all_gather(segment_ids, "ctx", axis=0, tiled=True)

    def backward_one_block(offset, size_each, inner_state):

        def backward_work(running):
            block_keys = lax.dynamic_slice_in_dim(backward_piece_keys, offset, size_each).reshape(
                size_each, heads_local, HDIM
            )
            block_values = lax.dynamic_slice_in_dim(
                backward_piece_values, offset, size_each
            ).reshape(size_each, heads_local, HDIM)
            block_seg = lax.dynamic_slice_in_dim(backward_piece_seg, offset, size_each)
            key_pos = offset + jnp.arange(size_each, dtype=jnp.int32)
            prob_low, grad_score = block_grads(
                query_heads,
                own_pos,
                segment_ids,
                grad_heads,
                lse_rows,
                delta_rows,
                block_keys,
                block_values,
                key_pos,
                block_seg,
                slopes,
            )
            query_acc = running[0] + jnp.einsum(
                "hqk,khd->qhd", grad_score, block_keys, preferred_element_type=jnp.float32
            ) / math.sqrt(HDIM)
            return (query_acc,)

        needed = (offset <= own_pos[-1]) & (
            seg_at(backward_piece_seg, offset + size_each - 1) >= own_first_seg
        )
        return lax.cond(needed, backward_work, lambda running: running, inner_state)

    back_result = over_blocks(backward_piece_keys.shape[0], backward_one_block, back_state)
    query_grad = back_result[0].reshape(local_rows, local_width)
    piece_query = lax.all_gather(query_rows, "ctx", axis=0, tiled=True)
    piece_grad = lax.all_gather(grad_attn, "ctx", axis=0, tiled=True)
    piece_lse = lax.all_gather(lse_rows.astype(jnp.bfloat16), "ctx", axis=0, tiled=True).astype(
        jnp.float32
    )
    piece_delta = lax.all_gather(delta_rows.astype(jnp.bfloat16), "ctx", axis=0, tiled=True).astype(
        jnp.float32
    )
    owner_piece_seg = lax.all_gather(segment_ids, "ctx", axis=0, tiled=True)

    def owner_one_block(offset, size_each, inner_state):

        def owner_work(running):
            key_acc, value_acc = running
            block_query = lax.dynamic_slice_in_dim(piece_query, offset, size_each).reshape(
                size_each, heads_local, HDIM
            )
            block_grad = lax.dynamic_slice_in_dim(piece_grad, offset, size_each).reshape(
                size_each, heads_local, HDIM
            )
            block_lse = lax.dynamic_slice_in_dim(piece_lse, offset, size_each)
            block_delta = lax.dynamic_slice_in_dim(piece_delta, offset, size_each)
            block_seg = lax.dynamic_slice_in_dim(owner_piece_seg, offset, size_each)
            query_pos = offset + jnp.arange(size_each, dtype=jnp.int32)
            prob_low, grad_score = block_grads(
                block_query,
                query_pos,
                block_seg,
                block_grad,
                block_lse,
                block_delta,
                key_heads,
                value_heads,
                own_pos,
                segment_ids,
                slopes,
            )
            key_acc = key_acc + jnp.einsum(
                "hqk,qhd->khd", grad_score, block_query, preferred_element_type=jnp.float32
            ) / math.sqrt(HDIM)
            value_acc = value_acc + jnp.einsum(
                "hqk,qhd->khd", prob_low, block_grad, preferred_element_type=jnp.float32
            )
            return (key_acc, value_acc)

        needed = (offset + size_each - 1 >= own_pos[0]) & (
            seg_at(owner_piece_seg, offset) <= own_last_seg
        )
        return lax.cond(needed, owner_work, lambda running: running, inner_state)

    key_acc, value_acc = over_blocks(
        piece_query.shape[0], owner_one_block, (query_zero, query_zero)
    )
    key_grad = key_acc.reshape(local_rows, local_width)
    value_grad = value_acc.reshape(local_rows, local_width)
    query_low = query_grad.astype(jnp.bfloat16)
    key_low = key_grad.astype(jnp.bfloat16)
    value_low = value_grad.astype(jnp.bfloat16)
    grad_bqv = jnp.stack(
        (
            jnp.sum(query_low.astype(jnp.float32), axis=0),
            jnp.sum(value_low.astype(jnp.float32), axis=0),
        )
    )
    stacked_grads = jnp.stack((query_low, key_low, value_low))
    grad_qkv = jnp.einsum(
        "td,cte->cde", hidden_one, stacked_grads, preferred_element_type=jnp.float32
    )
    part_one = jnp.einsum("cte,cde->td", stacked_grads, w_qkv, preferred_element_type=jnp.float32)
    grad_in_norm, grad_gain_one, grad_bias_one = norm_backward(
        part_one, normed_one, inverse_one, ln1_gain, tp_rank, local_width
    )
    input_grad = (grad_middle + grad_in_norm).astype(jnp.bfloat16)
    reduced = (
        lax.psum_scatter(
            grad_gain_one.astype(jnp.bfloat16), "ctx", scatter_dimension=0, tiled=True
        ).astype(jnp.float32),
        lax.psum_scatter(
            grad_bias_one.astype(jnp.bfloat16), "ctx", scatter_dimension=0, tiled=True
        ).astype(jnp.float32),
        lax.psum_scatter(
            grad_qkv.astype(jnp.bfloat16), "ctx", scatter_dimension=1, tiled=True
        ).astype(jnp.float32),
        lax.psum_scatter(
            grad_bqv.astype(jnp.bfloat16), "ctx", scatter_dimension=1, tiled=True
        ).astype(jnp.float32),
        lax.psum_scatter(
            grad_wout.astype(jnp.bfloat16), "ctx", scatter_dimension=1, tiled=True
        ).astype(jnp.float32),
        lax.psum_scatter(
            grad_bout.astype(jnp.bfloat16), "ctx", scatter_dimension=0, tiled=True
        ).astype(jnp.float32),
        lax.psum_scatter(
            grad_gain_two.astype(jnp.bfloat16), "ctx", scatter_dimension=0, tiled=True
        ).astype(jnp.float32),
        lax.psum_scatter(
            grad_bias_two.astype(jnp.bfloat16), "ctx", scatter_dimension=0, tiled=True
        ).astype(jnp.float32),
        lax.psum_scatter(
            grad_up.astype(jnp.bfloat16), "ctx", scatter_dimension=0, tiled=True
        ).astype(jnp.float32),
        lax.psum_scatter(
            grad_bup.astype(jnp.bfloat16), "ctx", scatter_dimension=0, tiled=True
        ).astype(jnp.float32),
        lax.psum_scatter(
            grad_down.astype(jnp.bfloat16), "ctx", scatter_dimension=1, tiled=True
        ).astype(jnp.float32),
        lax.psum_scatter(
            grad_bdown.astype(jnp.bfloat16), "ctx", scatter_dimension=0, tiled=True
        ).astype(jnp.float32),
    )
    return (output.astype(jnp.bfloat16), input_grad) + tuple(reduced)


def swap_halves(first, second):
    lane = lax.broadcasted_iota(jnp.int32, first.shape, 1)
    low = lane < HALF
    return (
        jnp.where(low, first, pltpu.roll(second, HALF, 1)),
        jnp.where(low, pltpu.roll(first, HALF, 1), second),
    )


def unpack_pair(ref, index, first_row, count):
    one = ref[index, first_row : first_row + count, :].astype(jnp.float32)
    two = ref[index + 1, first_row : first_row + count, :].astype(jnp.float32)
    return jnp.concatenate(swap_halves(one, two), axis=0)


def pack_pair(ref, index, first_row, count, rows):
    one, two = swap_halves(rows[:count], rows[count:])
    ref[index, first_row : first_row + count, :] = one.astype(ref.dtype)
    ref[index + 1, first_row : first_row + count, :] = two.astype(ref.dtype)


def dot_of(left, right, left_dim, right_dim):
    return lax.dot_general(
        left, right, (((left_dim,), (right_dim,)), ((), ())), preferred_element_type=jnp.float32
    )


def put_halves(ref, rank, own_ref, other_ref):
    width = own_ref.shape[1]
    ref[:, pl.ds(pl.multiple_of(rank * width, width), width)] = own_ref[...]
    ref[:, pl.ds(pl.multiple_of((1 - rank) * width, width), width)] = other_ref[...]


def put_stripes(ref, first_lane, turned_ref, chosen, order, value):
    side = 2 * HALF
    for number in range(1 << len(order)):
        source = 0
        for depth, bit in enumerate(order):
            source |= ((number >> (len(order) - 1 - depth)) & 1) << bit
        start = pl.multiple_of((source + (value << chosen)) * HALF, HALF)
        row, lane = (number * HALF) % side, first_lane + (number * HALF) // side * side
        ref[row : row + HALF, lane : lane + side] = turned_ref[pl.ds(start, HALF), :]


def qkv_kernel(
    rank_ref,
    place_ref,
    x_own_ref,
    x_other_ref,
    cot_own_ref,
    cot_other_ref,
    gain_ref,
    bias_ref,
    w_ref,
    b_ref,
    seg_ref,
    send_ref,
    x_ref,
    cot_ref,
    mine_ref,
    theirs_ref,
    h_ref,
    turn_ref,
):
    step = pl.program_id(0)
    rows, width = x_own_ref.shape
    heads = width // HDIM

    @pl.when(step == 0)
    def _():
        put_halves(x_ref, rank_ref[0], x_own_ref, x_other_ref)
        normed, _ = norm_stats(x_ref[...].astype(jnp.float32))
        h_ref[...] = (normed * gain_ref[...] + bias_ref[...]).astype(jnp.bfloat16)

    @pl.when(step == 2)
    def _():
        put_halves(cot_ref, rank_ref[0], cot_own_ref, cot_other_ref)
        turn_ref[...] = cot_ref[...].astype(jnp.float32).T.astype(jnp.bfloat16)
        bit = (place_ref[0] >> DOWN_BITS[0]) & 1
        put_stripes(mine_ref, 0, turn_ref, DOWN_BITS[0], DOWN_BITS[1:], bit)
        put_stripes(theirs_ref, 0, turn_ref, DOWN_BITS[0], DOWN_BITS[1:], 1 - bit)

    bias = jnp.where(step == 0, b_ref[0:1], jnp.where(step == 2, b_ref[1:2], 0.0))
    flat = jnp.dot(h_ref[...], w_ref[0], preferred_element_type=jnp.float32) + bias
    turned = flat.T

    @pl.when(step == 0)
    def _():
        scaled = turned.astype(jnp.bfloat16).astype(jnp.float32) * (1.0 / math.sqrt(HDIM))
        seg_rows = jnp.broadcast_to(seg_ref[...].astype(jnp.float32), (16, rows)).astype(
            jnp.bfloat16
        )
        for head in range(heads):
            pack_pair(send_ref, 2 * head, 2 * HDIM, HDIM // 2, scaled[head * HDIM : (head + 1) * HDIM])
            send_ref[2 * head, SEG_ROW : SEG_ROW + 16, :] = seg_rows
            send_ref[2 * head + 1, SEG_ROW : SEG_ROW + 16, :] = seg_rows

    for which in (1, 2):

        @pl.when(step == which)
        def _(which=which):
            low = turned.astype(jnp.bfloat16)
            for head in range(heads):
                piece = low[head * HDIM : (head + 1) * HDIM]
                send_ref[2 * head, (which - 1) * HDIM : which * HDIM, :] = piece
                send_ref[2 * head + 1, (which - 1) * HDIM : which * HDIM, :] = piece


def masked_scores(keys, query, slope, query_pos, begin, first_key, top):
    score = dot_of(keys, query, 1, 0)
    key_pos = first_key + lax.broadcasted_iota(jnp.int32, score.shape, 0)
    score = score + slope * (key_pos - top).astype(jnp.float32)
    allowed = (key_pos <= query_pos) & (key_pos >= begin)
    return jnp.where(allowed, score, mask_fill)


def doc_starts(recv_ref):
    seg = recv_ref[:, SEG_ROW : SEG_ROW + 16, :].astype(jnp.float32)[:, 0, :]
    one = jnp.sum(jnp.where(seg < 0.5, 1.0, 0.0))
    two = jnp.sum(jnp.where(seg < 1.5, 1.0, 0.0))
    return one.astype(jnp.int32), two.astype(jnp.int32)


def query_geometry(tile, place, starts):
    lane = lax.broadcasted_iota(jnp.int32, (1, QUERIES), 1)
    query_pos = 2 * HALF * (tile * SOURCES + lane // HALF) + HALF * place + lane % HALF
    begin_one, begin_two = starts
    begin = jnp.where(
        query_pos >= begin_two, begin_two, jnp.where(query_pos >= begin_one, begin_one, 0)
    )
    return query_pos, begin


def tile_rows(ref, tile, first_row):
    return jnp.concatenate(
        [
            unpack_pair(ref, tile * SOURCES + pair, first_row, HDIM // 2)
            for pair in range(0, SOURCES, 2)
        ],
        axis=1,
    )


def put_rows(ref, *pieces):
    first = 0
    for piece in pieces:
        ref[first : first + piece.shape[0], :] = piece[...]
        first += piece.shape[0]


def forward_kernel(
    slope_ref,
    place_ref,
    recv_ref,
    tokens_ref,
    far_ref,
    near_ref,
    corner_ref,
    send_ref,
    out_ref,
    lse_ref,
    joined_ref,
    key_ref,
):
    put_rows(joined_ref, tokens_ref, far_ref, near_ref, corner_ref)
    count = recv_ref.shape[0]
    block = 2 * HALF
    slope, place = slope_ref[0], place_ref[0]
    starts = doc_starts(recv_ref)
    for source in range(count):
        key_ref[source * block : (source + 1) * block, :] = (
            recv_ref[source, 0:HDIM, :].astype(jnp.float32).T.astype(jnp.bfloat16)
        )
    values = jnp.concatenate([recv_ref[s, HDIM : 2 * HDIM, :] for s in range(count)], axis=1)
    for tile in range(count // SOURCES):
        reach = (tile + 1) * SOURCES * block
        query = tile_rows(recv_ref, tile, 2 * HDIM).astype(jnp.bfloat16)
        query_pos, begin = query_geometry(tile, place, starts)
        score = masked_scores(key_ref[0:reach, :], query, slope, query_pos, begin, 0, reach)
        high = jnp.max(score, axis=0, keepdims=True)
        weights = jnp.exp(score - high)
        total = jnp.sum(weights, axis=0, keepdims=True)
        out = dot_of(values[:, 0:reach], weights.astype(jnp.bfloat16), 1, 0) / total
        here = slice(tile * QUERIES, (tile + 1) * QUERIES)
        out_ref[:, here] = out
        lse_ref[:, here] = high + jnp.log(total)
        for pair in range(0, SOURCES, 2):
            pack_pair(
                send_ref,
                tile * SOURCES + pair,
                0,
                HDIM // 2,
                out[:, pair * HALF : (pair + 2) * HALF],
            )


def heads_of(ref, first_row):
    return jnp.concatenate(
        [unpack_pair(ref, index, first_row, HDIM // 2) for index in range(0, ref.shape[0], 2)],
        axis=0,
    )


def out_kernel(rank_ref, recv_ref, w_ref, b_ref, part_ref, attn_ref, acc_ref):
    width = w_ref.shape[0]
    turned = heads_of(recv_ref, 0).astype(jnp.bfloat16)
    attn_ref[...] = turned
    acc_ref[...] = dot_of(turned, w_ref[...], 0, 0)
    own = pl.ds(pl.multiple_of(rank_ref[0] * width, width), width)
    acc_ref[:, own] = acc_ref[:, own] + b_ref[...]
    part_ref[...] = acc_ref[...].astype(jnp.bfloat16)


def gelu_pair(value):
    inner = GELU_A * (value + GELU_B * (value * value * value))
    tanh = jnp.tanh(inner)
    half = 0.5 * (1.0 + tanh)
    slope = half + 0.5 * value * (1.0 - tanh * tanh) * (
        GELU_A * (1.0 + 3.0 * GELU_B * (value * value))
    )
    return value * half, slope


def mlp_kernel(
    rank_ref,
    place_ref,
    x_ref,
    cot_ref,
    own_ref,
    other_ref,
    gain_ref,
    bias_ref,
    up_ref,
    b_up_ref,
    down_ref,
    line_ref,
    line_x_ref,
    attn_ref,
    middle_ref,
    act_ref,
    back_ref,
    mine_ref,
    b_grad_ref,
    share_ref,
    swap_ref,
    joined_ref,
    hidden_ref,
    turn_ref,
    grad_acc,
    mlp_acc,
):
    step = pl.program_id(0)
    rows = act_ref.shape[0]
    width = share_ref.shape[1]

    @pl.when(step == 0)
    def _():
        middle = (
            x_ref[...].astype(jnp.float32)
            + own_ref[...].astype(jnp.float32)
            + other_ref[...].astype(jnp.float32)
        )
        middle_ref[...] = middle
        normed, _ = norm_stats(middle.astype(jnp.bfloat16).astype(jnp.float32))
        hidden_ref[...] = (normed * gain_ref[...] + bias_ref[...]).astype(jnp.bfloat16)
        put_rows(joined_ref, line_ref, line_x_ref)
        turn_ref[...] = hidden_ref[...].astype(jnp.float32).T.astype(jnp.bfloat16)
        bit = (place_ref[0] >> UP_BITS[0]) & 1
        put_stripes(mine_ref, 0, turn_ref, UP_BITS[0], UP_BITS[1:], bit)
        first = back_ref.shape[1] - mine_ref.shape[1] - width
        put_stripes(back_ref, first, turn_ref, UP_BITS[0], UP_BITS[1:], 1 - bit)
        first += mine_ref.shape[1]
        for part in range(0, width, rows):
            back_ref[:, first + part : first + part + rows] = attn_ref[part : part + rows, :]
        grad_acc[...] = jnp.zeros_like(grad_acc)
        mlp_acc[...] = jnp.zeros_like(mlp_acc)

    pre = jnp.dot(hidden_ref[...], up_ref[...], preferred_element_type=jnp.float32) + b_up_ref[...]
    act, slope = gelu_pair(pre)
    act = act.astype(jnp.bfloat16)
    act_ref[...] = act
    grad_act = dot_of(cot_ref[...], down_ref[...], 1, 1)
    grad_pre = (grad_act * slope).astype(jnp.bfloat16)
    chunk = grad_pre.shape[1]
    back_ref[:, pl.ds(pl.multiple_of(step * chunk, chunk), chunk)] = grad_pre
    b_grad_ref[...] = jnp.sum(grad_pre.astype(jnp.float32), axis=0, keepdims=True)
    grad_acc[...] += dot_of(grad_pre, up_ref[...], 1, 1)
    mlp_acc[...] += jnp.dot(act, down_ref[...], preferred_element_type=jnp.float32)

    @pl.when(step == pl.num_programs(0) - 1)
    def _():
        rank = rank_ref[0]
        swap_ref[:, 0 : 2 * width] = grad_acc[...].astype(jnp.bfloat16)
        swap_ref[:, 2 * width :] = mlp_acc[
            :, pl.ds(pl.multiple_of((1 - rank) * width, width), width)
        ].astype(jnp.bfloat16)
        share_ref[...] = mlp_acc[:, pl.ds(pl.multiple_of(rank * width, width), width)]


def norm_back(whole, normed, inverse, gain):
    scaled = whole * gain
    mean_one = jnp.mean(scaled, axis=-1, keepdims=True)
    mean_two = jnp.mean(scaled * normed, axis=-1, keepdims=True)
    return inverse * (scaled - mean_one - normed * mean_two)


def middle_kernel(
    rank_ref,
    place_ref,
    cot_ref,
    own_ref,
    other_ref,
    middle_ref,
    share_ref,
    gain_ref,
    b_down_ref,
    w_out_ref,
    mixed_ref,
    grad_ref,
    send_ref,
    mine_ref,
    theirs_ref,
    small_ref,
    wide_ref,
    turn_ref,
):
    rows, width = mixed_ref.shape
    own = pl.ds(pl.multiple_of(rank_ref[0] * width, width), width)
    mixed_ref[...] = (
        middle_ref[:, own]
        + share_ref[...]
        + other_ref[:, 2 * width :].astype(jnp.float32)
        + b_down_ref[...]
    ).astype(jnp.bfloat16)
    whole = own_ref[:, 0 : 2 * width].astype(jnp.float32) + other_ref[:, 0 : 2 * width].astype(
        jnp.float32
    )
    normed, inverse = norm_stats(middle_ref[...].astype(jnp.bfloat16).astype(jnp.float32))
    cot = cot_ref[...].astype(jnp.float32)
    grad = cot + norm_back(whole, normed, inverse, gain_ref[...])
    low = grad.astype(jnp.bfloat16)
    turn_ref[...] = grad.T.astype(jnp.bfloat16)
    bit = (place_ref[0] >> UP_BITS[0]) & 1
    put_stripes(mine_ref, 0, turn_ref, UP_BITS[0], UP_BITS[1:], bit)
    put_stripes(theirs_ref, 0, turn_ref, UP_BITS[0], UP_BITS[1:], 1 - bit)
    wide_ref[0:1] = jnp.sum(whole * normed, axis=0, keepdims=True)
    wide_ref[1:2] = jnp.sum(whole, axis=0, keepdims=True)
    wide_ref[2:3] = jnp.sum(grad, axis=0, keepdims=True)
    wide_ref[3:4] = jnp.sum(cot, axis=0, keepdims=True)
    wide_ref[8:, :] = grad
    small_ref[...] = wide_ref[0:8, own]
    grad_ref[...] = wide_ref[8:, own]
    back = dot_of(w_out_ref[...], low, 1, 1).astype(jnp.bfloat16).astype(jnp.float32)
    for head in range(width // HDIM):
        pack_pair(send_ref, 2 * head, 0, HDIM // 2, back[head * HDIM : (head + 1) * HDIM])


def backward_kernel(
    slope_ref,
    place_ref,
    recv_ref,
    grad_ref,
    out_ref,
    lse_ref,
    send_ref,
    low_ref,
    key_ref,
    value_ref,
    key_acc,
    value_acc,
):
    count = recv_ref.shape[0]
    block = 2 * HALF
    slope, place = slope_ref[0], place_ref[0]
    starts = doc_starts(recv_ref)
    for source in range(count):
        there = slice(source * block, (source + 1) * block)
        key_ref[there, :] = recv_ref[source, 0:HDIM, :].astype(jnp.float32).T.astype(jnp.bfloat16)
        value_ref[there, :] = (
            recv_ref[source, HDIM : 2 * HDIM, :].astype(jnp.float32).T.astype(jnp.bfloat16)
        )
    keys_turned = jnp.concatenate([recv_ref[s, 0:HDIM, :] for s in range(count)], axis=1)
    key_acc[...] = jnp.zeros_like(key_acc)
    value_acc[...] = jnp.zeros_like(value_acc)
    for tile in range(count // SOURCES):
        reach = (tile + 1) * SOURCES * block
        here = slice(tile * QUERIES, (tile + 1) * QUERIES)
        query = tile_rows(recv_ref, tile, 2 * HDIM).astype(jnp.bfloat16)
        grad_wide = tile_rows(grad_ref, tile, 0)
        grad = grad_wide.astype(jnp.bfloat16)
        delta = jnp.sum(grad_wide * out_ref[:, here], axis=0, keepdims=True)
        query_pos, begin = query_geometry(tile, place, starts)
        score = masked_scores(key_ref[0:reach, :], query, slope, query_pos, begin, 0, reach)
        prob = jnp.exp(score - lse_ref[:, here])
        grad_prob = dot_of(value_ref[0:reach, :], grad, 1, 0)
        grad_score = (prob * (grad_prob - delta)).astype(jnp.bfloat16)
        key_acc[:, 0:reach] += dot_of(query, grad_score, 1, 1)
        value_acc[:, 0:reach] += dot_of(grad, prob.astype(jnp.bfloat16), 1, 1)
        query_grad = dot_of(keys_turned[:, 0:reach], grad_score, 1, 0) * (1.0 / math.sqrt(HDIM))
        query_grad = query_grad.astype(jnp.bfloat16).astype(jnp.float32)
        for pair in range(0, SOURCES, 2):
            index = tile * SOURCES + pair
            piece = query_grad[:, pair * HALF : (pair + 2) * HALF]
            pack_pair(send_ref, index, 2 * HDIM, HDIM // 2, piece)
            other = pltpu.roll(piece, HALF, 1)
            lane = lax.broadcasted_iota(jnp.int32, piece.shape, 1)
            mine = lane // HALF == place
            is_low = place == 0
            low_ref[0:HDIM, index * block : (index + 1) * block] = jnp.where(
                mine, jnp.where(is_low, piece, other), 0.0
            ).astype(jnp.bfloat16)
            low_ref[0:HDIM, (index + 1) * block : (index + 2) * block] = jnp.where(
                mine, jnp.where(is_low, other, piece), 0.0
            ).astype(jnp.bfloat16)
    low_ref[HDIM : 2 * HDIM, :] = key_acc[...].astype(jnp.bfloat16)
    low_ref[2 * HDIM :, :] = value_acc[...].astype(jnp.bfloat16)
    for source in range(count):
        there = slice(source * block, (source + 1) * block)
        send_ref[source, 0 : 2 * HDIM, :] = low_ref[HDIM:, there]


def weight_kernel(
    rank_ref, device_ref, gain_ref, bias_ref, grad_ref, *refs
):
    own_refs, other_refs = refs[:2], refs[2:4]
    send_ref, wide_ref, order_ref, acc_ref = refs[4:]
    block = 2 * HALF
    first = 0
    for own_ref, other_ref in zip(own_refs, other_refs):
        put_halves(wide_ref.at[first : first + own_ref.shape[0]], rank_ref[0], own_ref, other_ref)
        first += own_ref.shape[0]
    for position, code in enumerate(GATHERED):
        source = device_ref[0] ^ code
        order_ref[:, position * block : (position + 1) * block] = grad_ref[
            :, pl.ds(pl.multiple_of(source * block, block), block)
        ]
    acc_ref[...] = jnp.zeros_like(acc_ref)

    def add(step, carry):
        here = pl.ds(pl.multiple_of(step * 2 * block, 2 * block), 2 * block)
        normed, _ = norm_stats(wide_ref[here, :].astype(jnp.float32))
        hidden = (normed * gain_ref[...] + bias_ref[...]).astype(jnp.bfloat16)
        acc_ref[...] += jnp.dot(order_ref[:, here], hidden, preferred_element_type=jnp.float32)
        return carry

    lax.fori_loop(0, first // (2 * block), add, 0)
    for index in range(0, send_ref.shape[0], 2):
        pack_pair(
            send_ref, index, 0, 3 * HDIM // 2, acc_ref[:, index * HALF : (index + 2) * HALF]
        )


def hidden_kernel(recv_ref, w_ref, part_ref, b_ref, acc_ref):
    step = pl.program_id(0)
    count = recv_ref.shape[0]

    @pl.when(step == 0)
    def _():
        acc_ref[...] = jnp.zeros_like(acc_ref)

    def add(turned):
        acc_ref[...] += dot_of(turned, w_ref[0], 0, 1)
        ones = jnp.ones((8, turned.shape[1]), jnp.bfloat16)
        b_ref[0] = dot_of(ones, turned, 1, 1)

    @pl.when(step == 0)
    def _():
        add(heads_of(recv_ref, 2 * HDIM).astype(jnp.bfloat16))

    for which in (1, 2):

        @pl.when(step == which)
        def _(which=which):
            span = slice((which - 1) * HDIM, which * HDIM)
            add(
                jnp.concatenate(
                    [
                        recv_ref[index, span, :].astype(jnp.float32)
                        + recv_ref[index + 1, span, :].astype(jnp.float32)
                        for index in range(0, count, 2)
                    ],
                    axis=0,
                ).astype(jnp.bfloat16)
            )

    @pl.when(step == 2)
    def _():
        part_ref[...] = acc_ref[...].astype(jnp.bfloat16)


def input_kernel(rank_ref, x_ref, own_ref, other_ref, gain_ref, grad_ref, out_ref, small_ref, wide_ref):
    rows, width = out_ref.shape
    own = pl.ds(pl.multiple_of(rank_ref[0] * width, width), width)
    normed, inverse = norm_stats(x_ref[...].astype(jnp.float32))
    whole = own_ref[...].astype(jnp.float32) + other_ref[...].astype(jnp.float32)
    wide_ref[0:1] = jnp.sum(whole * normed, axis=0, keepdims=True)
    wide_ref[1:2] = jnp.sum(whole, axis=0, keepdims=True)
    wide_ref[8:, :] = norm_back(whole, normed, inverse, gain_ref[...])
    small_ref[...] = wide_ref[0:8, own]
    out_ref[...] = (grad_ref[...] + wide_ref[8:, own]).astype(jnp.bfloat16)


def call(
    kernel,
    outs,
    ins,
    scratch=(),
    grid=None,
    in_specs=None,
    out_specs=None,
    after=(),
    mebibytes=16,
    flops=10**8,
):
    vmem = pl.BlockSpec(memory_space=pltpu.VMEM)
    smem = pl.BlockSpec(memory_space=pltpu.SMEM)
    specs = list(in_specs or [smem if value.ndim == 1 else vmem for value in ins])
    options = {} if grid is None else {"grid": grid}
    taken = len(ins)
    waits = len(after)

    def body(*refs):
        kernel(*refs[:taken], *refs[taken + waits :])

    return pl.pallas_call(
        body,
        out_shape=[jax.ShapeDtypeStruct(shape, dtype) for shape, dtype in outs],
        in_specs=specs + [pl.BlockSpec(memory_space=pl.ANY)] * waits,
        out_specs=out_specs or [vmem] * len(outs),
        scratch_shapes=list(scratch),
        compiler_params=pltpu.CompilerParams(vmem_limit_bytes=mebibytes * 1024 * 1024),
        cost_estimate=pl.CostEstimate(
            flops=flops // 10**4, bytes_accessed=1024, transcendentals=0
        ),
        **options,
    )(*ins, *after)


def stripe_rows(ref, first, count):
    side = 2 * HALF
    blocks = [
        ref[:, pl.ds(pl.multiple_of(first + part * side, side), side)]
        for part in range(count // side)
    ]
    return jnp.concatenate(blocks, axis=0)


def wide_product(bit, piece, left_ref, left_got_ref, right_ref, right_got_ref):
    turned, columns, got_first = piece
    half = left_ref.shape[1] // 2
    if turned:
        first, tokens = right_got_ref.shape[1] - columns, right_ref.shape[1]
        right = jnp.concatenate(
            [
                jnp.concatenate(
                    [
                        right_ref[part : part + tokens, :],
                        right_got_ref[:, first + part : first + part + tokens],
                    ],
                    axis=1,
                )
                for part in range(0, columns, tokens)
            ],
            axis=0,
        )
    else:
        right = jnp.concatenate([right_ref[:, 0:columns], right_got_ref[:, 0:columns]], axis=0)
    left = jnp.concatenate(
        [
            stripe_rows(left_ref, bit * half, half),
            stripe_rows(left_got_ref, got_first + bit * half, half),
        ],
        axis=1,
    )
    return dot_of(left, right, 1, 1 if turned else 0)


def group_products(groups, place_ref, ins, wanted):
    at = 0
    for number, (order, pieces) in enumerate(groups):
        bit = bit_at(place_ref, order[1])
        first = 0
        for piece in pieces:
            here = slice(first, first + piece[1])
            first = here.stop
            yield number, here, wide_product(
                bit if wanted else 1 - bit, piece, *ins[4 * at : 4 * at + 4]
            )
            at += 1


def split_rows(bit, acc_ref, send_ref, keep_ref):
    half = keep_ref.shape[0]
    send_ref[...] = acc_ref[pl.ds(pl.multiple_of((1 - bit) * half, half), half), :].astype(
        send_ref.dtype
    )
    keep_ref[...] = acc_ref[pl.ds(pl.multiple_of(bit * half, half), half), :].astype(
        keep_ref.dtype
    )


def bit_at(place_ref, bit):
    return (place_ref[0] >> bit) & 1


def product_kernel(groups, place_ref, *refs):
    kinds = len(groups)
    for number, here, value in group_products(groups, place_ref, refs[:-kinds], False):
        refs[number - kinds][:, here] = value.astype(jnp.bfloat16)


def product_add_kernel(groups, place_ref, *refs):
    kinds = len(groups)
    got, sends, keeps, accs = (
        refs[first * kinds : (first + 1) * kinds or None] for first in range(-4, 0)
    )
    for number, here, value in group_products(groups, place_ref, refs[: -4 * kinds], True):
        accs[number][:, here] = value + got[number][:, here].astype(jnp.float32)
    for number, (order, _) in enumerate(groups):
        split_rows(bit_at(place_ref, order[2]), accs[number], sends[number], keeps[number])


def add_kernel(groups, place_ref, *refs):
    kinds = len(groups)
    send_ref, keep_ref, acc_ref = refs[2 * kinds :]
    first = 0
    for number in range(kinds):
        here = slice(first, first + refs[number].shape[1])
        first = here.stop
        acc_ref[:, here] = refs[number][...].astype(jnp.float32) + refs[kinds + number][
            ...
        ].astype(jnp.float32)
    split_rows(bit_at(place_ref, groups[0][0][3]), acc_ref, send_ref, keep_ref)


def last_kernel(keep_ref, got_ref, *out_refs):
    first = 0
    for ref in out_refs:
        here = slice(first, first + ref.shape[1])
        first = here.stop
        ref[...] = keep_ref[:, here].astype(jnp.float32) + got_ref[:, here].astype(jnp.float32)


def held(value, after):
    return pl.pallas_call(
        lambda *refs: None,
        out_shape=jax.ShapeDtypeStruct(value.shape, value.dtype),
        in_specs=[pl.BlockSpec(memory_space=pl.ANY)] * (1 + len(after)),
        out_specs=pl.BlockSpec(memory_space=pl.ANY),
        input_output_aliases={0: 0},
    )(value, *after)


def swap_over(value, bit, count):
    return lax.ppermute(value, "ctx", [(place, place ^ (1 << bit)) for place in range(count)])


class Reductions:
    def __init__(self, groups, device, count, ins):
        self.groups, self.device, self.count, self.ins = groups, device, count, ins
        self.columns = [sum(piece[1] for piece in pieces) for _, pieces in groups]
        self.rows = ins[0].shape[1] // 2

    def shapes(self, rows, dtype):
        return [((rows, columns), dtype) for columns in self.columns]

    def swap(self, sent, stage):
        return [
            swap_over(value, order[stage], self.count)
            for value, (order, _) in zip(sent, self.groups)
        ]

    def first(self, after):
        sent = call(
            functools.partial(product_kernel, self.groups),
            self.shapes(self.rows, jnp.bfloat16),
            [self.device] + self.ins,
            after=after,
            mebibytes=60,
            flops=10**15,
        )
        self.got = self.swap(sent, 1)
        return sent

    def second(self, after):
        half = self.rows // 2
        kinds = len(self.groups)
        results = call(
            functools.partial(product_add_kernel, self.groups),
            self.shapes(half, jnp.bfloat16) * 2,
            [self.device] + self.ins + self.got,
            scratch=[pltpu.VMEM((self.rows, columns), jnp.float32) for columns in self.columns],
            after=after,
            mebibytes=60,
            flops=10**15,
        )
        self.keep = results[kinds:]
        self.got = self.swap(results[:kinds], 2)
        return results[:kinds]

    def third(self, after):
        quarter = self.rows // 4
        wide = sum(self.columns)
        sent, self.keep = call(
            functools.partial(add_kernel, self.groups),
            [((quarter, wide), jnp.bfloat16)] * 2,
            [self.device] + list(self.keep) + list(self.got),
            scratch=[pltpu.VMEM((2 * quarter, wide), jnp.float32)],
            after=after,
            mebibytes=60,
            flops=2 * 10**9,
        )
        self.got = swap_over(sent, self.groups[0][0][3], self.count)
        return [sent]

    def last(self):
        return call(
            last_kernel,
            [
                ((self.rows // 4, piece[1]), jnp.float32)
                for _, pieces in self.groups
                for piece in pieces
            ],
            [self.keep, self.got],
            mebibytes=60,
            flops=10**9,
        )


def on_device_paired(
    tokens,
    segment_ids,
    ln1_gain,
    ln1_bias,
    w_qkv,
    b_qv,
    w_out,
    b_out,
    ln2_gain,
    ln2_bias,
    w_up,
    b_up,
    w_down,
    b_down,
    cotangent,
    count,
):
    bf16, f32 = jnp.bfloat16, jnp.float32
    rows, width = tokens.shape
    model = w_out.shape[1]
    hidden = w_up.shape[1]
    heads = width // HDIM
    block = 2 * HALF
    all_tokens = count * rows
    tp_rank = lax.axis_index("tp")
    place = lax.axis_index("ctx")
    rank = tp_rank.reshape(1)
    side = (place % 2).reshape(1)
    slope = head_slopes(tp_rank * heads + place // 2, 1)
    gain_one, bias_one = ln1_gain.reshape(1, model), ln1_bias.reshape(1, model)
    gain_two, bias_two = ln2_gain.reshape(1, model), ln2_bias.reshape(1, model)
    other_core = lambda value: lax.ppermute(value, "tp", [(0, 1), (1, 0)])
    to_heads = lambda value: lax.all_to_all(value, "ctx", 0, 0, tiled=True)
    smem = pl.BlockSpec(memory_space=pltpu.SMEM)
    whole = lambda *shape: pl.BlockSpec(shape, lambda step: (0,) * len(shape))

    device = place.reshape(1)
    sent, full_in, full_cot, cot_mine, cot_theirs = call(
        qkv_kernel,
        [
            ((count, FWD_ROWS, rows), bf16),
            ((rows, model), bf16),
            ((rows, model), bf16),
            ((rows, model // 2), bf16),
            ((rows, model // 2), bf16),
        ],
        [
            rank,
            device,
            tokens,
            other_core(tokens),
            cotangent,
            other_core(cotangent),
            gain_one,
            bias_one,
            w_qkv,
            b_qv,
            segment_ids.reshape(1, rows),
        ],
        scratch=[pltpu.VMEM((rows, model), bf16), pltpu.VMEM((model, rows), bf16)],
        grid=(3,),
        in_specs=[smem, smem]
        + [whole(rows, width)] * 4
        + [
            whole(1, model),
            whole(1, model),
            pl.BlockSpec((1, model, width), lambda step: (step, 0, 0)),
            whole(2, width),
            whole(1, rows),
        ],
        out_specs=[
            whole(count, FWD_ROWS, rows),
            whole(rows, model),
            whole(rows, model),
            whole(rows, model // 2),
            whole(rows, model // 2),
        ],
        mebibytes=60,
        flops=3 * 10**9,
    )
    cot_got = swap_over(cot_theirs, DOWN_BITS[0], count)
    bit_x, bit_y, bit_z, bit_far = range(4)
    far, near = swap_over(tokens, bit_far, count), swap_over(tokens, bit_z, count)
    corner = swap_over(far, bit_z, count)
    got = to_heads(held(sent, [far, near]))
    attn_sent, attn_raw, lse, line = call(
        forward_kernel,
        [
            ((count, HDIM // 2, rows), bf16),
            ((HDIM, all_tokens // 2), f32),
            ((1, all_tokens // 2), f32),
            ((4 * rows, width), bf16),
        ],
        [slope, side, got, tokens, far, near, corner],
        scratch=[pltpu.VMEM((all_tokens, HDIM), bf16)],
        after=[cot_got],
        mebibytes=24,
        flops=4 * 10**9,
    )
    line_x = swap_over(line, bit_x, count)
    attn_got = to_heads(attn_sent)
    part, attn_turned = call(
        out_kernel,
        [((rows, model), bf16), ((width, rows), bf16)],
        [rank, attn_got, w_out, b_out.reshape(1, width)],
        scratch=[pltpu.VMEM((rows, model), f32)],
    )
    chunk = 512
    middle, act, grad_pre, h_mine, grad_b_up, share, swap, plane = call(
        mlp_kernel,
        [
            ((rows, model), f32),
            ((rows, hidden), bf16),
            ((rows, hidden + model // 2 + width), bf16),
            ((rows, model // 2), bf16),
            ((1, hidden), f32),
            ((rows, width), f32),
            ((rows, model + width), bf16),
            ((8 * rows, width), bf16),
        ],
        [
            rank,
            device,
            full_in,
            full_cot,
            part,
            other_core(part),
            gain_two,
            bias_two,
            w_up,
            b_up.reshape(1, hidden),
            w_down,
            line,
            line_x,
            attn_turned,
        ],
        grid=(hidden // chunk,),
        in_specs=[smem, smem]
        + [whole(rows, model)] * 4
        + [
            whole(1, model),
            whole(1, model),
            pl.BlockSpec((model, chunk), lambda step: (0, step)),
            pl.BlockSpec((1, chunk), lambda step: (0, step)),
            pl.BlockSpec((chunk, model), lambda step: (step, 0)),
            whole(4 * rows, width),
            whole(4 * rows, width),
            whole(width, rows),
        ],
        out_specs=[
            whole(rows, model),
            pl.BlockSpec((rows, chunk), lambda step: (0, step)),
            whole(rows, hidden + model // 2 + width),
            whole(rows, model // 2),
            pl.BlockSpec((1, chunk), lambda step: (0, step)),
            whole(rows, width),
            whole(rows, model + width),
            whole(8 * rows, width),
        ],
        scratch=[
            pltpu.VMEM((rows, model), bf16),
            pltpu.VMEM((model, rows), bf16),
            pltpu.VMEM((rows, model), f32),
            pltpu.VMEM((rows, model), f32),
        ],
        mebibytes=56,
        flops=7 * 10**9,
    )
    gathered = [plane, swap_over(plane, bit_y, count)]
    gathered += [other_core(value) for value in gathered]
    mixed, grad_mid, grad_sent, low_mine, out_theirs, small_two = call(
        middle_kernel,
        [
            ((rows, width), bf16),
            ((rows, width), f32),
            ((count, HDIM // 2, rows), bf16),
            ((rows, model // 2), bf16),
            ((rows, model // 2), bf16),
            ((8, width), f32),
        ],
        [
            rank,
            device,
            full_cot,
            swap,
            other_core(swap),
            middle,
            share,
            gain_two,
            b_down.reshape(1, width),
            w_out,
        ],
        scratch=[pltpu.VMEM((rows + 8, model), f32), pltpu.VMEM((model, rows), bf16)],
        mebibytes=60,
        flops=2 * 10**9,
    )
    back_other = swap_over(grad_pre, UP_BITS[0], count)
    reductions = Reductions(
        (
            (DOWN_BITS, ((False, hidden, 0),)),
            (UP_BITS, ((False, hidden, hidden), (True, width, 0))),
        ),
        device,
        count,
        [cot_mine, cot_got, act, swap_over(act, DOWN_BITS[0], count)]
        + [h_mine, back_other, grad_pre, back_other]
        + [low_mine, swap_over(out_theirs, UP_BITS[0], count)]
        + [attn_turned, back_other],
    )
    grad_got = to_heads(grad_sent)
    first_sent = reductions.first([grad_got, gathered[1]])
    back_sent, back_low = call(
        backward_kernel,
        [((count, SEG_ROW, rows), bf16), ((3 * HDIM, all_tokens), bf16)],
        [slope, side, got, grad_got, attn_raw, lse],
        scratch=[
            pltpu.VMEM((all_tokens, HDIM), bf16),
            pltpu.VMEM((all_tokens, HDIM), bf16),
            pltpu.VMEM((HDIM, all_tokens), f32),
            pltpu.VMEM((HDIM, all_tokens), f32),
        ],
        after=[first_sent[0]] + gathered[2:],
        mebibytes=56,
        flops=10**10,
    )
    (weight_sent,) = call(
        weight_kernel,
        [((count, 3 * HDIM // 2, rows), bf16)],
        [rank, device, gain_one, bias_one, back_low] + gathered,
        scratch=[
            pltpu.VMEM((all_tokens, model), bf16),
            pltpu.VMEM((3 * HDIM, all_tokens), bf16),
            pltpu.VMEM((3 * HDIM, model), f32),
        ],
        mebibytes=56,
        flops=6 * 10**9,
    )
    weight_got = to_heads(weight_sent)
    second_sent = reductions.second([weight_sent])
    third_sent = reductions.third([])
    back_got = to_heads(back_sent)
    part_one, sums = call(
        hidden_kernel,
        [
            ((rows, model), bf16),
            ((3, 8, width), f32),
        ],
        [back_got, w_qkv],
        grid=(3,),
        in_specs=[
            whole(count, SEG_ROW, rows),
            pl.BlockSpec((1, model, width), lambda step: (step, 0, 0)),
        ],
        out_specs=[
            whole(rows, model),
            pl.BlockSpec((1, 8, width), lambda step: (step, 0, 0)),
        ],
        scratch=[pltpu.VMEM((rows, model), f32)],
        after=[second_sent[0]],
        flops=3 * 10**9,
    )
    input_grad, small_one = call(
        input_kernel,
        [((rows, width), bf16), ((8, width), f32)],
        [rank, full_in, part_one, other_core(part_one), gain_one, grad_mid],
        scratch=[pltpu.VMEM((rows + 8, model), f32)],
        after=[third_sent[0]],
    )
    grad_down, grad_up, grad_out = reductions.last()
    stripe = model // count
    grad_qkv = (
        weight_got.astype(f32)
        .reshape(heads, 2, 3 * HDIM // 2, 2 * stripe)
        .sum(axis=1)
        .reshape(heads, 3 * HDIM // 2, 2, stripe)
        .transpose(0, 2, 1, 3)
        .reshape(heads, 3, HDIM, stripe)
        .transpose(1, 3, 0, 2)
        .reshape(3, stripe, width)
    )
    share_w = width // count
    vectors = jnp.concatenate(
        [
            small_one[0:2].reshape(2, count, share_w),
            sums[0:3:2, 0].reshape(2, count, share_w),
            small_two[0:4].reshape(4, count, share_w),
            grad_b_up.reshape(count, -1, share_w).transpose(1, 0, 2),
        ],
        axis=0,
    )
    lanes = vectors.shape[0] * share_w
    spread = vectors.transpose(1, 0, 2).reshape(count, 1, lanes)
    total = jnp.sum(to_heads(spread), axis=0).reshape(-1, share_w)
    return (
        mixed,
        input_grad,
        total[0],
        total[1],
        grad_qkv,
        total[2:4],
        grad_out.T,
        total[6],
        total[4],
        total[5],
        grad_up,
        total[8:].reshape(-1),
        grad_down.T,
        total[7],
    )


def paired(mesh, arrays):
    sizes = dict(mesh.shape)
    count, cores = sizes["ctx"], sizes["tp"]
    rows = arrays[0].shape[0] // count
    return (
        cores == 2
        and count == 16
        and rows == 2 * HALF
        and count * cores == 2 * HEADS
        and arrays[0].shape[1] == HEADS * HDIM
    )


def solution(mesh):
    in_specs = (
        P("ctx", "tp"),
        P("ctx"),
        P(),
        P(),
        P(None, None, "tp"),
        P(None, "tp"),
        P("tp", None),
        P("tp"),
        P(),
        P(),
        P(None, "tp"),
        P("tp"),
        P("tp", None),
        P("tp"),
        P("ctx", "tp"),
    )
    out_specs = (
        P("ctx", "tp"),
        P("ctx", "tp"),
        P(("tp", "ctx")),
        P(("tp", "ctx")),
        P(None, "ctx", "tp"),
        P(None, ("tp", "ctx")),
        P("tp", "ctx"),
        P(("tp", "ctx")),
        P(("tp", "ctx")),
        P(("tp", "ctx")),
        P("ctx", "tp"),
        P(("tp", "ctx")),
        P("tp", "ctx"),
        P(("tp", "ctx")),
    )

    def run(*arrays):
        if paired(mesh, arrays):
            body = functools.partial(on_device_paired, count=dict(mesh.shape)["ctx"])
        else:
            body = on_device
        return jax.shard_map(
            body, mesh=mesh, in_specs=in_specs, out_specs=out_specs, check_vma=False
        )(*arrays)

    return run
```
